32 devices in a mesh: seq: 8 (over z, core), head: 4 (over y, x).
Axes of the slice: x: 2, y: 2, z: 4, core: 2. Of those that a mesh axis runs over, the one named last changes fastest.
Arguments:
- features: bfloat16 [8192, 8192], P(('seq', 'head')), may hold values from -6 to 6
- step_size: float32 [8192, 128], P(('seq', 'head')), may hold values from 0.01 to 0.08
- log_decay: float32 [8192, 128], P(('seq', 'head')), may hold values from -0.6 to 0
- inject: bfloat16 [8192, 1024], P(('seq', 'head')), may hold values from -1.5 to 1.5
- readout: bfloat16 [8192, 1024], P(('seq', 'head')), may hold values from -1.5 to 1.5
- skip_gain: float32 [128], replicated, may hold values from 0.5 to 1.5
Outputs:
- mixer_out: bfloat16 [8192, 8192], P(('seq', 'head'))
The draws below stay inside these ranges and needn't reach their ends.
All inputs are finite; a program needn't handle non-finite values.
Results may differ from the reference program's by a relative error of at most 0.02.
Values may be sent and summed in bfloat16 or wider, within the bound.
A program may use at most 128 MiB of HBM per device.

```python
import math
import jax
import jax.numpy as jnp
from jax import lax

MIXER_HEADS = 128
HEAD_DIM = 64
STATE = 128
GROUPS = 8
SPAN = 512
TOK_DEV = 256
TOKENS = 8192


def draw_log_decay(key, part):
    random_subkeys = jax.random.split(key, 7)
    fast_share = 0.5
    fast_heads = jax.random.uniform(random_subkeys[0], (MIXER_HEADS,), jnp.float32) < fast_share
    fast_rate = jnp.exp(jax.random.uniform(random_subkeys[1], (MIXER_HEADS,), jnp.float32, math.log(1.0 / 50.0), math.log(1.0 / 25.0)))
    slow_rate = jnp.exp(jax.random.uniform(random_subkeys[2], (MIXER_HEADS,), jnp.float32, math.log(0.3), math.log(0.6))) / TOKENS
    head_rate = jnp.where(fast_heads, fast_rate, slow_rate)
    block_count = TOKENS // TOK_DEV
    factor = jnp.exp(jax.random.uniform(random_subkeys[3], (block_count, 1), jnp.float32, math.log(0.5), math.log(2.0)))
    factor = jnp.repeat(factor, TOK_DEV, axis=0)
    roughness = jax.random.uniform(random_subkeys[4], (TOKENS, MIXER_HEADS), jnp.float32, 0.5, 1.5)
    baseline_portion = -head_rate[None, :] * factor * roughness
    token_positions = jax.random.randint(random_subkeys[5], (3,), 0, TOKENS)
    surge_length = jax.random.uniform(random_subkeys[6], (3, MIXER_HEADS), jnp.float32, 0.22, 0.45)
    token_identifiers = jnp.arange(TOKENS, dtype=jnp.int32)
    surge_selected = (token_identifiers[:, None] == token_positions[None, :]).astype(jnp.float32)
    surge_portion = jnp.sum(surge_selected[:, :, None] * surge_length[None, :, :], axis=1)
    return (baseline_portion - surge_portion).astype(jnp.float32)


def levels(key, extent, cuts, low, high):
    loudness, own = 1.0, jax.random.fold_in(key, 6)
    for axis_at, shards_of in cuts:
        draws = jnp.exp(jax.random.uniform(jax.random.fold_in(own, axis_at), (shards_of,), jnp.float32, low / len(cuts), high / len(cuts)))
        loudness = loudness * jnp.repeat(draws, extent[axis_at] // shards_of).reshape([-1 if axis == axis_at else 1 for axis in range(len(extent))])
    return loudness


def bell_draw(key, extent, deviation, most, shards=(), kind=jnp.bfloat16):
    loudness = levels(key, extent, shards, -0.22, 0.18) if shards else 1.0
    values = jax.random.normal(key, extent, jnp.float32) * deviation * loudness
    return jnp.minimum(jnp.maximum(values, -most), most).astype(kind)


def setup_inputs(seed: int = 0) -> dict:
    key_of = jax.random.split(jax.random.key(seed), 7)
    features = bell_draw(key_of[0], (TOKENS, MIXER_HEADS * HEAD_DIM), 1.0, 6.0, ((0, 32),))
    step_size = jnp.clip(jnp.exp(math.log(0.08) - 2.0794415 * jax.random.uniform(key_of[1], (TOKENS, MIXER_HEADS), jnp.float32) ** levels(key_of[1], (TOKENS, MIXER_HEADS), ((0, 32),), -0.2, 0.2)), 0.01, 0.08)
    log_decay = draw_log_decay(jax.random.fold_in(key_of[6], 71), 0)
    inject = bell_draw(key_of[3], (TOKENS, GROUPS * STATE), 0.25, 1.5, ((0, 32),))
    readout = bell_draw(key_of[4], (TOKENS, GROUPS * STATE), 0.25, 1.5, ((0, 32),))
    skip_gain = jnp.clip(jax.random.uniform(key_of[5], (MIXER_HEADS,), jnp.float32, 0.5, 1.5), 0.5, 1.5)
    return {"features": features, "step_size": step_size, "log_decay": log_decay, "inject": inject, "readout": readout, "skip_gain": skip_gain}


def reference(features, step_size, log_decay, inject, readout, skip_gain):
    length = features.shape[0]
    spans = length // SPAN
    per_group = MIXER_HEADS // GROUPS
    drive = (features.reshape(length, MIXER_HEADS, HEAD_DIM).astype(jnp.float32) * step_size[:, :, None]).astype(jnp.bfloat16)
    cum_all = jnp.cumsum(log_decay.reshape(spans, SPAN, MIXER_HEADS), axis=1)
    inject_q = inject.reshape(spans, SPAN, GROUPS, STATE)
    readout_q = readout.reshape(spans, SPAN, GROUPS, STATE)
    drive_q = drive.reshape(spans, SPAN, GROUPS, per_group, HEAD_DIM)
    plain_q = features.reshape(spans, SPAN, GROUPS, per_group, HEAD_DIM)
    row_ids = lax.broadcasted_iota(jnp.int32, (SPAN, SPAN), 0)
    col_ids = lax.broadcasted_iota(jnp.int32, (SPAN, SPAN), 1)
    lower_mask = row_ids >= col_ids
    gains = skip_gain.reshape(GROUPS, per_group)

    def advance(carried, pieces):
        read_c, inject_c, drive_c, cum_c, plain_c = pieces
        read_f = read_c.astype(jnp.float32)
        inject_f = inject_c.astype(jnp.float32)
        drive_f = drive_c.astype(jnp.float32)
        intersection = jnp.einsum("ign,jgn->gij", read_f, inject_f)
        cum_heads = cum_c.T
        log_gap = cum_heads[:, :, None] - cum_heads[:, None, :]
        decays = jnp.where(lower_mask, jnp.exp(jnp.where(lower_mask, log_gap, 0.0)), 0.0)
        weights = (decays.reshape(GROUPS, per_group, SPAN, SPAN) * intersection[:, None]).astype(jnp.bfloat16)
        inner_out = jnp.einsum("ghij,jghp->ighp", weights.astype(jnp.float32), drive_f)
        held = carried.astype(jnp.bfloat16).astype(jnp.float32).reshape(GROUPS, per_group, HEAD_DIM, STATE)
        outer_out = jnp.einsum("ign,ghpn->ighp", read_f, held) * jnp.exp(cum_c).reshape(SPAN, GROUPS, per_group)[..., None]
        tail_decay = jnp.exp(cum_heads[:, -1:] - cum_heads)
        scaled = (drive_f * tail_decay.T.reshape(SPAN, GROUPS, per_group)[..., None]).astype(jnp.bfloat16)
        summary = jnp.einsum("jghp,jgn->ghpn", scaled.astype(jnp.float32), inject_f).reshape(MIXER_HEADS, HEAD_DIM, STATE)
        updated = carried * jnp.exp(cum_heads[:, -1])[:, None, None] + summary
        total_out = inner_out + outer_out + gains[None, :, :, None] * plain_c.astype(jnp.float32)
        return updated, total_out.astype(jnp.bfloat16).reshape(SPAN, MIXER_HEADS * HEAD_DIM)

    start_state = jnp.zeros((MIXER_HEADS, HEAD_DIM, STATE), jnp.float32)
    final_state, outputs = lax.scan(advance, start_state, (readout_q, inject_q, drive_q, cum_all, plain_q))
    return outputs.reshape(length, MIXER_HEADS * HEAD_DIM)
```

```python
import functools

import jax
import jax.numpy as jnp
from jax import lax
from jax.experimental import pallas as pl
from jax.experimental.pallas import tpu as pltpu
from jax.sharding import PartitionSpec as P

HEAD_DIM = 64
STATE = 128
GROUPS = 8
CHUNK = 128
F32 = jnp.float32
BF16 = jnp.bfloat16


def dot(a, b):
    return jnp.dot(a, b, preferred_element_type=F32)


def dot_rows(a, b):
    return lax.dot_general(a, b, (((0,), (0,)), ((), ())), preferred_element_type=F32)


def dot_last(a, b):
    return lax.dot_general(a, b, (((1,), (1,)), ((), ())), preferred_element_type=F32)


def lower(size):
    return lax.broadcasted_iota(jnp.int32, (size, size), 0) >= lax.broadcasted_iota(
        jnp.int32, (size, size), 1
    )


def cumulative(decay):
    ones = jnp.where(lower(CHUNK), 1.0, 0.0).astype(BF16)
    high = decay.astype(BF16)
    rest = decay - high.astype(F32)
    mid = rest.astype(BF16)
    low = (rest - mid.astype(F32)).astype(BF16)
    return dot(ones, high) + dot(ones, mid) + dot(ones, low)


def split(x):
    high = x.astype(BF16)
    return jnp.concatenate([high, (x - high.astype(F32)).astype(BF16)], axis=1)


def spread(group, heads, columns):
    head = lax.broadcasted_iota(jnp.int32, (2 * heads, columns), 0)
    head = jnp.where(head >= heads, head - heads, head)
    column = lax.broadcasted_iota(jnp.int32, (2 * heads, columns), 1)
    first = (head - group * (columns // HEAD_DIM)) * HEAD_DIM
    return jnp.where((column >= first) & (column < first + HEAD_DIM), 1.0, 0.0).astype(BF16)


def factors(step_ref, decay_ref):
    half = CHUNK // 2 - 1
    out = []
    for c in range(2):
        rows = pl.ds(c * CHUNK, CHUNK)
        cum = cumulative(decay_ref[rows, :])
        mid, end = cum[half : half + 1], cum[CHUNK - 1 : CHUNK]
        out.append((step_ref[rows, :] * jnp.exp(mid - cum), jnp.exp(cum - mid), mid, end))
    return out


def pad8(rows):
    rows = list(rows)
    return jnp.concatenate(rows + [jnp.zeros_like(rows[0])] * (16 - len(rows)), axis=0)


def summary_kernel(x_ref, step_ref, decay_ref, inject_ref, state_ref, total_ref, fac):
    heads = step_ref.shape[1]
    group = pl.program_id(0)

    @pl.when(group == 0)
    def _():
        (u0, _, m0, e0), (u1, _, m1, e1) = factors(step_ref, decay_ref)
        fac[...] = split(
            jnp.concatenate([u0, u1, pad8([jnp.exp(e0 - m0 + e1), jnp.exp(e1 - m1)])], axis=0)
        )
        total_ref[...] = e0 + e1

    wide = dot(fac[...], spread(group, heads, x_ref.shape[1]))
    state = None
    for c in range(2):
        rows = slice(c * CHUNK, (c + 1) * CHUNK)
        drive = (wide[rows] * x_ref[rows, :].astype(F32)).astype(BF16)
        part = dot_rows(inject_ref[rows, :], drive) * wide[2 * CHUNK + c : 2 * CHUNK + c + 1]
        state = part if state is None else state + part
    state_ref[...] = state.astype(BF16)


def output_kernel(
    x_ref, step_ref, decay_ref, inject_ref, readout_ref, skip_ref, held_ref, out_ref, fac
):
    heads = step_ref.shape[1]
    group = pl.program_id(0)

    @pl.when(group == 0)
    def _():
        (u0, w0, m0, e0), (u1, w1, m1, e1) = factors(step_ref, decay_ref)
        aux = [jnp.exp(m0), jnp.exp(m1 + e0), jnp.exp(m1 + e0 - m0), skip_ref[...]]
        fac[...] = split(jnp.concatenate([u0, u1, w0, w1, pad8(aux)], axis=0))

    wide = dot(fac[...], spread(group, heads, x_ref.shape[1]))
    aux = 4 * CHUNK
    held = held_ref[...].astype(F32)
    mask = lower(CHUNK)
    enter = held * wide[aux : aux + 1]
    for c in range(2):
        rows = slice(c * CHUNK, (c + 1) * CHUNK)
        x = x_ref[rows, :].astype(F32)
        drive = (wide[rows] * x).astype(BF16)
        inject, readout = inject_ref[rows, :], readout_ref[rows, :]
        cross = jnp.where(mask, dot_last(readout, inject), 0.0).astype(BF16)
        left = jnp.concatenate([cross, readout], axis=1)
        right = jnp.concatenate([drive, enter.astype(BF16)], axis=0)
        acc = dot(left, right)
        after = wide[(2 + c) * CHUNK : (3 + c) * CHUNK]
        out_ref[rows, :] = (after * acc + wide[aux + 3 : aux + 4] * x).astype(BF16)
        if c == 0:
            enter = held * wide[aux + 1 : aux + 2] + dot_rows(inject, drive) * wide[aux + 2 : aux + 3]


def shards(features, step_size, log_decay, inject, readout, skip_gain):
    ways, place = lax.axis_size("head"), lax.axis_index("head")
    seq_place, seq_ways = lax.axis_index("seq"), lax.axis_size("seq")
    tokens, width = features.shape
    heads = step_size.shape[1]
    block = width // GROUPS
    params = pltpu.CompilerParams(vmem_limit_bytes=48 * 2**20)
    wide_spec = pl.BlockSpec((tokens, block), lambda g: (0, g))
    full = pl.BlockSpec((tokens, heads), lambda g: (0, 0))
    group_spec = pl.BlockSpec((tokens, STATE), lambda g: (0, g))
    state_spec = pl.BlockSpec((STATE, block), lambda g: (0, g))
    row_spec = pl.BlockSpec((1, heads), lambda g: (0, 0))
    state, total = pl.pallas_call(
        summary_kernel,
        grid=(GROUPS,),
        in_specs=[wide_spec, full, full, group_spec],
        out_specs=[state_spec, row_spec],
        out_shape=[
            jax.ShapeDtypeStruct((STATE, width), BF16),
            jax.ShapeDtypeStruct((1, heads), F32),
        ],
        scratch_shapes=[pltpu.VMEM((2 * CHUNK + 16, 2 * heads), BF16)],
        compiler_params=params,
    )(features, step_size, log_decay, inject)

    totals = lax.all_gather(total[0], ("seq", "head")).reshape(seq_ways, ways, heads)
    own_heads = heads // ways
    mine = lax.dynamic_slice_in_dim(totals, place * own_heads, own_heads, 2)
    parts = lax.all_to_all(
        state.reshape(STATE, ways, width // ways), "head", split_axis=1, concat_axis=0, tiled=True
    ).reshape(ways, STATE, own_heads, HEAD_DIM).astype(F32)
    local = lax.dynamic_index_in_dim(mine, seq_place, 0, False)
    running = jnp.zeros(parts.shape[1:], F32)
    before, decays = [], []
    gone = jnp.zeros((own_heads,), F32)
    for j in range(ways):
        before.append(running)
        decays.append(gone)
        running = running * jnp.exp(local[j])[None, :, None] + parts[j]
        gone = gone + local[j]
    gathered = lax.all_gather(running.astype(BF16), "seq")
    seq_total = mine.sum(1)
    enter = jnp.zeros_like(running)
    for s in range(seq_ways):
        step = enter * jnp.exp(seq_total[s])[None, :, None] + gathered[s].astype(F32)
        enter = jnp.where(s < seq_place, step, enter)
    back = jnp.stack(
        [
            (enter * jnp.exp(decays[j])[None, :, None] + before[j]).astype(BF16)
            for j in range(ways)
        ]
    ).reshape(ways, STATE, width // ways)
    held = lax.all_to_all(back, "head", split_axis=0, concat_axis=2, tiled=True)[0]

    return pl.pallas_call(
        output_kernel,
        grid=(GROUPS,),
        in_specs=[wide_spec, full, full, group_spec, group_spec, row_spec, state_spec],
        out_specs=wide_spec,
        out_shape=jax.ShapeDtypeStruct((tokens, width), BF16),
        scratch_shapes=[pltpu.VMEM((4 * CHUNK + 16, 2 * heads), BF16)],
        compiler_params=params,
    )(features, step_size, log_decay, inject, readout, skip_gain[None], held)


def solution(mesh):
    rows = P(("seq", "head"), None)
    return jax.shard_map(
        shards,
        mesh=mesh,
        in_specs=(rows, rows, rows, rows, rows, P()),
        out_specs=rows,
        check_vma=False,
    )
```

```python
import functools

import jax
import jax.numpy as jnp
from jax import lax
from jax.experimental import pallas as pl
from jax.experimental.pallas import tpu as pltpu
from jax.sharding import PartitionSpec as P

HEAD_DIM = 64
STATE = 128
GROUPS = 8
CHUNK = 128
PIECE = 512
MESH = pl.DeviceIdType.MESH
F32 = jnp.float32
BF16 = jnp.bfloat16


def dot(a, b):
    return jnp.dot(a, b, preferred_element_type=F32)


def dot_rows(a, b):
    return lax.dot_general(a, b, (((0,), (0,)), ((), ())), preferred_element_type=F32)


def dot_last(a, b):
    return lax.dot_general(a, b, (((1,), (1,)), ((), ())), preferred_element_type=F32)


def lower(size):
    return lax.broadcasted_iota(jnp.int32, (size, size), 0) >= lax.broadcasted_iota(
        jnp.int32, (size, size), 1
    )


def cumulative(decay):
    ones = jnp.where(lower(CHUNK), 1.0, 0.0).astype(BF16)
    high = decay.astype(BF16)
    rest = decay - high.astype(F32)
    mid = rest.astype(BF16)
    low = (rest - mid.astype(F32)).astype(BF16)
    return dot(ones, high) + dot(ones, mid) + dot(ones, low)


def split(x):
    high = x.astype(BF16)
    return jnp.concatenate([high, (x - high.astype(F32)).astype(BF16)], axis=1)


def spread(group, heads, columns):
    head = lax.broadcasted_iota(jnp.int32, (2 * heads, columns), 0)
    head = jnp.where(head >= heads, head - heads, head)
    column = lax.broadcasted_iota(jnp.int32, (2 * heads, columns), 1)
    first = (head - group * (columns // HEAD_DIM)) * HEAD_DIM
    return jnp.where((column >= first) & (column < first + HEAD_DIM), 1.0, 0.0).astype(BF16)


def factors(step_ref, decay_ref):
    half = CHUNK // 2 - 1
    out = []
    for c in range(2):
        rows = pl.ds(c * CHUNK, CHUNK)
        cum = cumulative(decay_ref[rows, :])
        mid, end = cum[half : half + 1], cum[CHUNK - 1 : CHUNK]
        out.append((step_ref[rows, :] * jnp.exp(mid - cum), jnp.exp(cum - mid), mid, end))
    return out


def pad8(rows):
    rows = list(rows)
    return jnp.concatenate(rows + [jnp.zeros_like(rows[0])] * (16 - len(rows)), axis=0)


def scan_kernel(
    ways,
    seqs,
    x_ref,
    step_ref,
    decay_ref,
    inject_ref,
    held_ref,
    fac,
    tot,
    pair,
    dec,
    up_stage,
    parts,
    down_stage,
    total_stage,
    total_in,
    next_stage,
    enter_in,
    tot_send,
    tot_recv,
    pair_send,
    pair_recv,
    up_send,
    up_recv,
    down_send,
    down_recv,
    total_send,
    total_recv,
    next_send,
    enter_recv,
    keep_sem,
):
    heads = step_ref.shape[1]
    width = x_ref.shape[1]
    own = width // ways
    depth = own // PIECE
    me, seq = lax.axis_index("head"), lax.axis_index("seq")
    core, chip = lax.rem(seq, 2), seq // 2
    chips = seqs // 2
    first = chip == 0

    def peer(q):
        return (seq, q)

    def other(i):
        return lax.rem(me + i, ways)

    def remote(src, dst, send, recv, device):
        return pltpu.make_async_remote_copy(
            src_ref=src,
            dst_ref=dst,
            send_sem=send,
            recv_sem=recv,
            device_id=device,
            device_id_type=MESH,
        )

    barrier = pltpu.get_barrier_semaphore()

    def greet(device):
        pl.semaphore_signal(barrier, inc=1, device_id=device, device_id_type=MESH)

    for i in range(1, ways):
        greet(peer(other(i)))

    @pl.when(core == 1)
    def _():
        greet((seq - 1, me))

    @pl.when((core == 1) & (chip > 0))
    def _():
        greet((seq - 2, me))

    @pl.when((core == 0) & (chip > 0))
    def _():
        greet((seq - 1, me))

    (u0, _, m0, e0), (u1, _, m1, e1) = factors(step_ref, decay_ref)
    fac[...] = split(
        jnp.concatenate([u0, u1, pad8([jnp.exp(e0 - m0 + e1), jnp.exp(e1 - m1)])], axis=0)
    )
    tot[me] = jnp.broadcast_to(e0 + e1, (8, heads))

    @pl.when(first)
    def _():
        enter_in[...] = jnp.zeros_like(enter_in)

    ahead = 2 - 2 * (chip // (chips - 1)) if chips > 1 else 0
    pl.semaphore_wait(barrier, ways - core + core * ahead)

    def tot_copy(q):
        return remote(tot.at[me], tot.at[me], tot_send.at[q], tot_recv.at[me], peer(q))

    def tot_from(q):
        return remote(tot.at[q], tot.at[q], tot_send.at[q], tot_recv.at[q], peer(q))

    def up_copy(k, q):
        return remote(
            up_stage.at[k, q], parts.at[k, me], up_send.at[k, q], up_recv.at[k, me], peer(q)
        )

    def up_from(k, q):
        return remote(
            up_stage.at[k, q], parts.at[k, q], up_send.at[k, q], up_recv.at[k, q], peer(q)
        )

    def down_copy(k, q):
        return remote(
            down_stage.at[k, q],
            held_ref.at[me * depth + k],
            down_send.at[k, q],
            down_recv.at[k, me],
            peer(q),
        )

    def down_from(k, q):
        return remote(
            down_stage.at[k, q],
            held_ref.at[q * depth + k],
            down_send.at[k, q],
            down_recv.at[k, q],
            peer(q),
        )

    def keep_copy(k):
        return pltpu.make_async_copy(
            down_stage.at[k, me], held_ref.at[me * depth + k], keep_sem.at[k]
        )

    def pair_copy():
        return remote(pair.at[0], pair.at[1], pair_send, pair_recv, (seq + 1, me))

    def total_copy(k):
        return remote(
            total_stage.at[k], total_in.at[k], total_send.at[k], total_recv.at[k], (seq + 1, me)
        )

    def next_copy(k, ahead):
        return remote(
            next_stage.at[k],
            enter_in.at[k],
            next_send.at[k, ahead - 1],
            enter_recv.at[k],
            (seq + ahead, me),
        )

    for i in range(1, ways):
        tot_copy(other(i)).start()

    def piece(t, carry):
        k, i = t // ways, lax.rem(t, ways)
        q = lax.rem(me + 1 + i, ways)
        index = q * depth + k
        columns = pl.ds(pl.multiple_of(index * PIECE, PIECE), PIECE)
        group = index * PIECE // (width // GROUPS)
        shared = pl.ds(pl.multiple_of(group * STATE, STATE), STATE)
        wide = dot(fac[...], spread(index, heads, PIECE))
        state = None
        for c in range(2):
            rows = slice(c * CHUNK, (c + 1) * CHUNK)
            drive = (wide[rows] * x_ref[rows, columns].astype(F32)).astype(BF16)
            part = dot_rows(inject_ref[rows, shared], drive)
            part = part * wide[2 * CHUNK + c : 2 * CHUNK + c + 1]
            state = part if state is None else state + part

        @pl.when(i == ways - 1)
        def _():
            parts[k, me] = state.astype(BF16)

        @pl.when(i < ways - 1)
        def _():
            up_stage[k, q] = state.astype(BF16)
            up_copy(k, q).start()

        return carry

    lax.fori_loop(0, depth * ways, piece, 0)

    for i in range(1, ways):
        tot_from(other(i)).wait_recv()
    logs = [tot[j][:1] for j in range(ways)]
    whole = sum(logs[1:], logs[0])

    @pl.when(core == 0)
    def _():
        pair[0] = jnp.broadcast_to(whole, (8, heads))
        pair_copy().start()
        pair[1] = jnp.zeros((8, heads), F32)

    @pl.when(core == 1)
    def _():
        pair_copy().wait_recv()

    rows = [jnp.exp(a) for a in logs] + [jnp.exp(pair[1][:1])]
    rows = split(jnp.concatenate(rows + [jnp.zeros_like(rows[0])] * (-len(rows) % 16), axis=0))
    for k in range(depth):
        dec[k] = dot(rows, spread(me * depth + k, heads, PIECE))

    def await_parts(k):
        for i in range(1, ways):
            up_from(k, other(i)).wait_recv()

    def onward(k, running, j):
        return running * dec[k, j : j + 1, :] + parts[k, j].astype(F32)

    def returns(k, running):
        for j in range(ways):
            down_stage[k, j] = running.astype(BF16)
            running = onward(k, running, j)
        return running

    def send_down(k):
        for i in range(1, ways):
            down_copy(k, other(i)).start()
        keep_copy(k).start()

    def await_enter(k):
        @pl.when(chip > 0)
        def _():
            next_copy(k, 1).wait_recv()

    @pl.when(core == 0)
    def _():
        def totals(k, carry):
            await_parts(k)
            running = parts[k, 0].astype(F32)
            for j in range(1, ways):
                running = onward(k, running, j)
            total_stage[k] = running.astype(BF16)
            total_copy(k).start()
            return carry

        def finish(k, carry):
            await_enter(k)
            returns(k, enter_in[k].astype(F32))
            send_down(k)
            return carry

        lax.fori_loop(0, depth, totals, 0)
        lax.fori_loop(0, depth, finish, 0)

    @pl.when(core == 1)
    def _():
        def finish(k, carry):
            await_parts(k)
            total_copy(k).wait_recv()
            await_enter(k)
            start = enter_in[k].astype(F32) * dec[k, ways : ways + 1, :]
            running = returns(k, start + total_in[k].astype(F32))

            @pl.when(chip < chips - 1)
            def _():
                next_stage[k] = running.astype(BF16)
                next_copy(k, 2).start()
                next_copy(k, 1).start()

            send_down(k)
            return carry

        lax.fori_loop(0, depth, finish, 0)

    def drain(k, carry):
        for i in range(1, ways):
            down_from(k, other(i)).wait_recv()
        for i in range(1, ways):
            up_copy(k, other(i)).wait_send()
            down_copy(k, other(i)).wait_send()
        keep_copy(k).wait()

        @pl.when(core == 0)
        def _():
            total_copy(k).wait_send()

        @pl.when((core == 1) & (chip < chips - 1))
        def _():
            next_copy(k, 2).wait_send()
            next_copy(k, 1).wait_send()

        return carry

    lax.fori_loop(0, depth, drain, 0)
    for i in range(1, ways):
        tot_copy(other(i)).wait_send()

    @pl.when(core == 0)
    def _():
        pair_copy().wait_send()


def output_kernel(
    x_ref, step_ref, decay_ref, inject_ref, readout_ref, skip_ref, held_ref, out_ref, fac
):
    heads = step_ref.shape[1]
    group = pl.program_id(0)

    @pl.when(group == 0)
    def _():
        (u0, w0, m0, e0), (u1, w1, m1, e1) = factors(step_ref, decay_ref)
        aux = [jnp.exp(m0), jnp.exp(m1 + e0), jnp.exp(m1 + e0 - m0), skip_ref[...]]
        fac[...] = split(jnp.concatenate([u0, u1, w0, w1, pad8(aux)], axis=0))

    wide = dot(fac[...], spread(group, heads, x_ref.shape[1]))
    aux = 4 * CHUNK
    held = jnp.concatenate([held_ref[i] for i in range(held_ref.shape[0])], axis=1).astype(F32)
    mask = lower(CHUNK)
    enter = held * wide[aux : aux + 1]
    for c in range(2):
        rows = slice(c * CHUNK, (c + 1) * CHUNK)
        x = x_ref[rows, :].astype(F32)
        drive = (wide[rows] * x).astype(BF16)
        inject, readout = inject_ref[rows, :], readout_ref[rows, :]
        cross = jnp.where(mask, dot_last(readout, inject), 0.0).astype(BF16)
        left = jnp.concatenate([cross, readout], axis=1)
        right = jnp.concatenate([drive, enter.astype(BF16)], axis=0)
        acc = dot(left, right)
        after = wide[(2 + c) * CHUNK : (3 + c) * CHUNK]
        out_ref[rows, :] = (after * acc + wide[aux + 3 : aux + 4] * x).astype(BF16)
        if c == 0:
            enter = held * wide[aux + 1 : aux + 2] + dot_rows(inject, drive) * wide[aux + 2 : aux + 3]


def shards(features, step_size, log_decay, inject, readout, skip_gain):
    ways, seqs = lax.axis_size("head"), lax.axis_size("seq")
    tokens, width = features.shape
    heads = step_size.shape[1]
    block = width // GROUPS
    depth = width // ways // PIECE
    params = pltpu.CompilerParams(vmem_limit_bytes=48 * 2**20)
    vmem = pl.BlockSpec(memory_space=pltpu.VMEM)
    dma = pltpu.SemaphoreType.DMA
    held = pl.pallas_call(
        functools.partial(scan_kernel, ways, seqs),
        in_specs=[vmem] * 4,
        out_specs=pl.BlockSpec(memory_space=pl.ANY),
        out_shape=jax.ShapeDtypeStruct((width // PIECE, STATE, PIECE), BF16),
        scratch_shapes=[
            pltpu.VMEM((2 * CHUNK + 16, 2 * heads), BF16),
            pltpu.VMEM((ways, 8, heads), F32),
            pltpu.VMEM((2, 8, heads), F32),
            pltpu.VMEM((depth, (ways + 16) // 16 * 16, PIECE), F32),
            pltpu.VMEM((depth, ways, STATE, PIECE), BF16),
            pltpu.VMEM((depth, ways, STATE, PIECE), BF16),
            pltpu.VMEM((depth, ways, STATE, PIECE), BF16),
            pltpu.VMEM((depth, STATE, PIECE), BF16),
            pltpu.VMEM((depth, STATE, PIECE), BF16),
            pltpu.VMEM((depth, STATE, PIECE), BF16),
            pltpu.VMEM((depth, STATE, PIECE), BF16),
            dma((ways,)),
            dma((ways,)),
            dma,
            dma,
            dma((depth, ways)),
            dma((depth, ways)),
            dma((depth, ways)),
            dma((depth, ways)),
            dma((depth,)),
            dma((depth,)),
            dma((depth, 2)),
            dma((depth,)),
            dma((depth,)),
        ],
        compiler_params=pltpu.CompilerParams(
            vmem_limit_bytes=48 * 2**20, collective_id=0, has_side_effects=True
        ),
    )(features, step_size, log_decay, inject)

    wide_spec = pl.BlockSpec((tokens, block), lambda g: (0, g))
    full = pl.BlockSpec((tokens, heads), lambda g: (0, 0))
    group_spec = pl.BlockSpec((tokens, STATE), lambda g: (0, g))
    state_spec = pl.BlockSpec((block // PIECE, STATE, PIECE), lambda g: (g, 0, 0))
    row_spec = pl.BlockSpec((1, heads), lambda g: (0, 0))
    return pl.pallas_call(
        output_kernel,
        grid=(GROUPS,),
        in_specs=[wide_spec, full, full, group_spec, group_spec, row_spec, state_spec],
        out_specs=wide_spec,
        out_shape=jax.ShapeDtypeStruct((tokens, width), BF16),
        scratch_shapes=[pltpu.VMEM((4 * CHUNK + 16, 2 * heads), BF16)],
        compiler_params=params,
    )(features, step_size, log_decay, inject, readout, skip_gain[None], held)


def solution(mesh):
    rows = P(("seq", "head"), None)
    return jax.shard_map(
        shards,
        mesh=mesh,
        in_specs=(rows, rows, rows, rows, rows, P()),
        out_specs=rows,
        check_vma=False,
    )
```

```python
import functools

import jax
import jax.numpy as jnp
from jax import lax
from jax.experimental import pallas as pl
from jax.experimental.pallas import tpu as pltpu
from jax.sharding import PartitionSpec as P

HEAD_DIM = 64
STATE = 128
GROUPS = 8
CHUNK = 128
PIECE = 512
MESH = pl.DeviceIdType.MESH
F32 = jnp.float32
BF16 = jnp.bfloat16


def dot(a, b):
    return jnp.dot(a, b, preferred_element_type=F32)


def dot_rows(a, b):
    return lax.dot_general(a, b, (((0,), (0,)), ((), ())), preferred_element_type=F32)


def dot_last(a, b):
    return lax.dot_general(a, b, (((1,), (1,)), ((), ())), preferred_element_type=F32)


def lower(size):
    return lax.broadcasted_iota(jnp.int32, (size, size), 0) >= lax.broadcasted_iota(
        jnp.int32, (size, size), 1
    )


def cumulative(decay):
    ones = jnp.where(lower(CHUNK), 1.0, 0.0).astype(BF16)
    high = decay.astype(BF16)
    rest = decay - high.astype(F32)
    mid = rest.astype(BF16)
    low = (rest - mid.astype(F32)).astype(BF16)
    return dot(ones, high) + dot(ones, mid) + dot(ones, low)


def split(x):
    high = x.astype(BF16)
    return jnp.concatenate([high, (x - high.astype(F32)).astype(BF16)], axis=1)


def spread(group, heads, columns):
    head = lax.broadcasted_iota(jnp.int32, (2 * heads, columns), 0)
    head = jnp.where(head >= heads, head - heads, head)
    column = lax.broadcasted_iota(jnp.int32, (2 * heads, columns), 1)
    first = (head - group * (columns // HEAD_DIM)) * HEAD_DIM
    return jnp.where((column >= first) & (column < first + HEAD_DIM), 1.0, 0.0).astype(BF16)


def factors(step_ref, decay_ref):
    half = CHUNK // 2 - 1
    out = []
    for c in range(2):
        rows = pl.ds(c * CHUNK, CHUNK)
        cum = cumulative(decay_ref[rows, :])
        mid, end = cum[half : half + 1], cum[CHUNK - 1 : CHUNK]
        out.append((step_ref[rows, :] * jnp.exp(mid - cum), jnp.exp(cum - mid), mid, end))
    return out


def pad8(rows):
    rows = list(rows)
    return jnp.concatenate(rows + [jnp.zeros_like(rows[0])] * (16 - len(rows)), axis=0)


def mixer_kernel(
    ways,
    seqs,
    x_hbm,
    step_hbm,
    decay_hbm,
    inject_hbm,
    readout_hbm,
    skip_ref,
    out_hbm,
    x_ref,
    step_ref,
    decay_ref,
    inject_ref,
    readout_ref,
    held_ref,
    drive_ref,
    first_state,
    after_ref,
    left_ref,
    fac,
    fac_out,
    tot,
    pair,
    dec,
    up_stage,
    parts,
    down_stage,
    total_stage,
    total_in,
    next_stage,
    enter_in,
    tot_send,
    tot_recv,
    pair_send,
    pair_recv,
    up_send,
    up_recv,
    down_send,
    down_recv,
    total_send,
    total_recv,
    next_send,
    enter_recv,
    keep_sem,
    load_sem,
    x_sem,
    out_sem,
):
    heads = step_ref.shape[1]
    width = x_ref.shape[1]
    own = width // ways
    depth = own // PIECE
    me, seq = lax.axis_index("head"), lax.axis_index("seq")
    core, chip = lax.rem(seq, 2), seq // 2
    chips = seqs // 2
    first = chip == 0

    def peer(q):
        return (seq, q)

    def other(i):
        return lax.rem(me + i, ways)

    def remote(src, dst, send, recv, device):
        return pltpu.make_async_remote_copy(
            src_ref=src,
            dst_ref=dst,
            send_sem=send,
            recv_sem=recv,
            device_id=device,
            device_id_type=MESH,
        )

    def load(i):
        src = (decay_hbm, step_hbm, inject_hbm, readout_hbm)[i]
        dst = (decay_ref, step_ref, inject_ref, readout_ref)[i]
        return pltpu.make_async_copy(src, dst, load_sem.at[i])

    def columns_of(index):
        return pl.ds(pl.multiple_of(index * PIECE, PIECE), PIECE)

    def load_x(index):
        columns = columns_of(index)
        return pltpu.make_async_copy(x_hbm.at[:, columns], x_ref.at[:, columns], x_sem.at[index])

    def store(index):
        columns = columns_of(index)
        return pltpu.make_async_copy(
            x_ref.at[:, columns], out_hbm.at[:, columns], out_sem.at[index]
        )

    def place(t):
        return lax.rem(me + 1 + lax.rem(t, ways), ways) * depth + t // ways

    for i in range(3):
        load(i).start()

    def begin(t, carry):
        load_x(place(t)).start()
        return carry

    lax.fori_loop(0, depth * ways, begin, 0)
    load(3).start()

    barrier = pltpu.get_barrier_semaphore()

    def greet(device):
        pl.semaphore_signal(barrier, inc=1, device_id=device, device_id_type=MESH)

    for i in range(1, ways):
        greet(peer(other(i)))

    @pl.when(core == 1)
    def _():
        greet((seq - 1, me))

    @pl.when((core == 1) & (chip > 0))
    def _():
        greet((seq - 2, me))

    @pl.when((core == 0) & (chip > 0))
    def _():
        greet((seq - 1, me))

    load(0).wait()
    load(1).wait()
    (u0, w0, m0, e0), (u1, w1, m1, e1) = factors(step_ref, decay_ref)
    fac[...] = split(
        jnp.concatenate([u0, u1, pad8([jnp.exp(e0 - m0 + e1), jnp.exp(e1 - m1)])], axis=0)
    )
    aux = [jnp.exp(m0), jnp.exp(m1 + e0), jnp.exp(m1 + e0 - m0), skip_ref[...]]
    fac_out[...] = split(jnp.concatenate([w0, w1, pad8(aux)], axis=0))
    tot[me] = jnp.broadcast_to(e0 + e1, (8, heads))

    @pl.when(first)
    def _():
        enter_in[...] = jnp.zeros_like(enter_in)

    ahead = 2 - 2 * (chip // (chips - 1)) if chips > 1 else 0
    pl.semaphore_wait(barrier, ways - core + core * ahead)

    def tot_copy(q):
        return remote(tot.at[me], tot.at[me], tot_send.at[q], tot_recv.at[me], peer(q))

    def tot_from(q):
        return remote(tot.at[q], tot.at[q], tot_send.at[q], tot_recv.at[q], peer(q))

    def up_copy(k, q):
        return remote(
            up_stage.at[k, q], parts.at[k, me], up_send.at[k, q], up_recv.at[k, me], peer(q)
        )

    def up_from(k, q):
        return remote(
            up_stage.at[k, q], parts.at[k, q], up_send.at[k, q], up_recv.at[k, q], peer(q)
        )

    def down_copy(k, q):
        return remote(
            down_stage.at[k, q],
            held_ref.at[me * depth + k],
            down_send.at[k, q],
            down_recv.at[k, me],
            peer(q),
        )

    def down_from(k, q):
        return remote(
            down_stage.at[k, q],
            held_ref.at[q * depth + k],
            down_send.at[k, q],
            down_recv.at[k, q],
            peer(q),
        )

    def keep_copy(k):
        return pltpu.make_async_copy(
            down_stage.at[k, me], held_ref.at[me * depth + k], keep_sem.at[k]
        )

    def pair_copy():
        return remote(pair.at[0], pair.at[1], pair_send, pair_recv, (seq + 1, me))

    def total_copy(k):
        return remote(
            total_stage.at[k], total_in.at[k], total_send.at[k], total_recv.at[k], (seq + 1, me)
        )

    def next_copy(k, ahead):
        return remote(
            next_stage.at[k],
            enter_in.at[k],
            next_send.at[k, ahead - 1],
            enter_recv.at[k],
            (seq + ahead, me),
        )

    for i in range(1, ways):
        tot_copy(other(i)).start()

    def piece(t, carry):
        k, i = t // ways, lax.rem(t, ways)
        q = lax.rem(me + 1 + i, ways)
        index = q * depth + k
        columns = columns_of(index)
        group = index * PIECE // (width // GROUPS)
        shared = pl.ds(pl.multiple_of(group * STATE, STATE), STATE)
        load_x(index).wait()
        wide = dot(fac[...], spread(index, heads, PIECE))
        state = None
        for c in range(2):
            rows = slice(c * CHUNK, (c + 1) * CHUNK)
            drive = (wide[rows] * x_ref[rows, columns].astype(F32)).astype(BF16)
            drive_ref[rows, columns] = drive
            part = dot_rows(inject_ref[rows, shared], drive)
            if c == 0:
                first_state[index] = part
            part = part * wide[2 * CHUNK + c : 2 * CHUNK + c + 1]
            state = part if state is None else state + part

        @pl.when(i == ways - 1)
        def _():
            parts[k, me] = state.astype(BF16)

        @pl.when(i < ways - 1)
        def _():
            up_stage[k, q] = state.astype(BF16)
            up_copy(k, q).start()

        return carry

    load(2).wait()
    lax.fori_loop(0, depth * ways, piece, 0)

    for i in range(1, ways):
        tot_from(other(i)).wait_recv()
    logs = [tot[j][:1] for j in range(ways)]
    whole = sum(logs[1:], logs[0])

    @pl.when(core == 0)
    def _():
        pair[0] = jnp.broadcast_to(whole, (8, heads))
        pair_copy().start()
        pair[1] = jnp.zeros((8, heads), F32)

    @pl.when(core == 1)
    def _():
        pair_copy().wait_recv()

    rows = [jnp.exp(a) for a in logs] + [jnp.exp(pair[1][:1])]
    rows = split(jnp.concatenate(rows + [jnp.zeros_like(rows[0])] * (-len(rows) % 16), axis=0))
    for k in range(depth):
        dec[k] = dot(rows, spread(me * depth + k, heads, PIECE))

    def await_parts(k):
        for i in range(1, ways):
            up_from(k, other(i)).wait_recv()

    def onward(k, running, j):
        return running * dec[k, j : j + 1, :] + parts[k, j].astype(F32)

    def returns(k, running):
        for j in range(ways):
            down_stage[k, j] = running.astype(BF16)
            running = onward(k, running, j)
        return running

    def send_down(k):
        for i in range(1, ways):
            down_copy(k, other(i)).start()
        keep_copy(k).start()

    def await_enter(k):
        @pl.when(chip > 0)
        def _():
            next_copy(k, 1).wait_recv()

    @pl.when(core == 0)
    def _():
        def totals(k, carry):
            await_parts(k)
            running = parts[k, 0].astype(F32)
            for j in range(1, ways):
                running = onward(k, running, j)
            total_stage[k] = running.astype(BF16)
            total_copy(k).start()
            return carry

        def finish(k, carry):
            await_enter(k)
            returns(k, enter_in[k].astype(F32))
            send_down(k)
            return carry

        lax.fori_loop(0, depth, totals, 0)
        lax.fori_loop(0, depth, finish, 0)

    @pl.when(core == 1)
    def _():
        def finish(k, carry):
            await_parts(k)
            total_copy(k).wait_recv()
            await_enter(k)
            start = enter_in[k].astype(F32) * dec[k, ways : ways + 1, :]
            running = returns(k, start + total_in[k].astype(F32))

            @pl.when(chip < chips - 1)
            def _():
                next_stage[k] = running.astype(BF16)
                next_copy(k, 2).start()
                next_copy(k, 1).start()

            send_down(k)
            return carry

        lax.fori_loop(0, depth, finish, 0)

    load(3).wait()
    mask = lower(CHUNK)

    def prepare(index, carry):
        columns = columns_of(index)
        after_ref[:, columns] = dot(fac_out[...], spread(index, heads, PIECE))
        return carry

    def cross(group, carry):
        shared = pl.ds(pl.multiple_of(group * STATE, STATE), STATE)
        for c in range(2):
            rows = slice(c * CHUNK, (c + 1) * CHUNK)
            readout = readout_ref[rows, shared]
            both = dot_last(readout, inject_ref[rows, shared])
            left_ref[group, rows, :CHUNK] = jnp.where(mask, both, 0.0).astype(BF16)
            left_ref[group, rows, CHUNK:] = readout
        return carry

    lax.fori_loop(0, GROUPS, cross, 0)
    lax.fori_loop(0, width // PIECE, prepare, 0)

    def result(k, q):
        index = q * depth + k
        columns = columns_of(index)
        group = index * PIECE // (width // GROUPS)
        held = held_ref[index].astype(F32)
        rest = after_ref[2 * CHUNK : 2 * CHUNK + 8, columns]
        enter = held * rest[0:1]
        for c in range(2):
            rows = slice(c * CHUNK, (c + 1) * CHUNK)
            right = jnp.concatenate([drive_ref[rows, columns], enter.astype(BF16)], axis=0)
            acc = dot(left_ref[group, rows, :], right)
            plain = rest[3:4] * x_ref[rows, columns].astype(F32)
            x_ref[rows, columns] = (after_ref[rows, columns] * acc + plain).astype(BF16)
            if c == 0:
                enter = held * rest[1:2] + first_state[index] * rest[2:3]
        store(index).start()

    def results(t, carry):
        k, i = t // ways, lax.rem(t, ways)
        q = lax.rem(me + i, ways)

        @pl.when(i == 0)
        def _():
            keep_copy(k).wait()

        @pl.when(i > 0)
        def _():
            down_from(k, q).wait_recv()

        result(k, q)
        return carry

    lax.fori_loop(0, depth * ways, results, 0)

    def drain(k, carry):
        for i in range(1, ways):
            up_copy(k, other(i)).wait_send()
            down_copy(k, other(i)).wait_send()

        @pl.when(core == 0)
        def _():
            total_copy(k).wait_send()

        @pl.when((core == 1) & (chip < chips - 1))
        def _():
            next_copy(k, 2).wait_send()
            next_copy(k, 1).wait_send()

        return carry

    lax.fori_loop(0, depth, drain, 0)

    def stored(index, carry):
        store(index).wait()
        return carry

    lax.fori_loop(0, width // PIECE, stored, 0)
    for i in range(1, ways):
        tot_copy(other(i)).wait_send()

    @pl.when(core == 0)
    def _():
        pair_copy().wait_send()


def shards(features, step_size, log_decay, inject, readout, skip_gain):
    ways, seqs = lax.axis_size("head"), lax.axis_size("seq")
    tokens, width = features.shape
    heads = step_size.shape[1]
    depth = width // ways // PIECE
    pieces = width // PIECE
    vmem = pl.BlockSpec(memory_space=pltpu.VMEM)
    dma = pltpu.SemaphoreType.DMA
    return pl.pallas_call(
        functools.partial(mixer_kernel, ways, seqs),
        in_specs=[pl.BlockSpec(memory_space=pl.ANY)] * 5 + [vmem],
        out_specs=pl.BlockSpec(memory_space=pl.ANY),
        out_shape=jax.ShapeDtypeStruct((tokens, width), BF16),
        scratch_shapes=[
            pltpu.VMEM((tokens, width), BF16),
            pltpu.VMEM((tokens, heads), F32),
            pltpu.VMEM((tokens, heads), F32),
            pltpu.VMEM((tokens, GROUPS * STATE), BF16),
            pltpu.VMEM((tokens, GROUPS * STATE), BF16),
            pltpu.VMEM((pieces, STATE, PIECE), BF16),
            pltpu.VMEM((tokens, width), BF16),
            pltpu.VMEM((pieces, STATE, PIECE), F32),
            pltpu.VMEM((tokens + 16, width), F32),
            pltpu.VMEM((GROUPS, tokens, CHUNK + STATE), BF16),
            pltpu.VMEM((2 * CHUNK + 16, 2 * heads), BF16),
            pltpu.VMEM((2 * CHUNK + 16, 2 * heads), BF16),
            pltpu.VMEM((ways, 8, heads), F32),
            pltpu.VMEM((2, 8, heads), F32),
            pltpu.VMEM((depth, (ways + 16) // 16 * 16, PIECE), F32),
            pltpu.VMEM((depth, ways, STATE, PIECE), BF16),
            pltpu.VMEM((depth, ways, STATE, PIECE), BF16),
            pltpu.VMEM((depth, ways, STATE, PIECE), BF16),
            pltpu.VMEM((depth, STATE, PIECE), BF16),
            pltpu.VMEM((depth, STATE, PIECE), BF16),
            pltpu.VMEM((depth, STATE, PIECE), BF16),
            pltpu.VMEM((depth, STATE, PIECE), BF16),
            dma((ways,)),
            dma((ways,)),
            dma,
            dma,
            dma((depth, ways)),
            dma((depth, ways)),
            dma((depth, ways)),
            dma((depth, ways)),
            dma((depth,)),
            dma((depth,)),
            dma((depth, 2)),
            dma((depth,)),
            dma((depth,)),
            dma((4,)),
            dma((pieces,)),
            dma((pieces,)),
        ],
        compiler_params=pltpu.CompilerParams(
            vmem_limit_bytes=60 * 2**20, collective_id=0, has_side_effects=True
        ),
    )(features, step_size, log_decay, inject, readout, skip_gain[None])


def solution(mesh):
    rows = P(("seq", "head"), None)
    return jax.shard_map(
        shards,
        mesh=mesh,
        in_specs=(rows, rows, rows, rows, rows, P()),
        out_specs=rows,
        check_vma=False,
    )
```

```python
import functools

import jax
import jax.numpy as jnp
from jax import lax
from jax.experimental import pallas as pl
from jax.experimental.pallas import tpu as pltpu
from jax.sharding import PartitionSpec as P

HEAD_DIM = 64
STATE = 128
GROUPS = 8
CHUNK = 128
PIECE = 256
MESH = pl.DeviceIdType.MESH
F32 = jnp.float32
BF16 = jnp.bfloat16


def dot(a, b):
    return jnp.dot(a, b, preferred_element_type=F32)


def dot_rows(a, b):
    return lax.dot_general(a, b, (((0,), (0,)), ((), ())), preferred_element_type=F32)


def dot_last(a, b):
    return lax.dot_general(a, b, (((1,), (1,)), ((), ())), preferred_element_type=F32)


def lower(size):
    return lax.broadcasted_iota(jnp.int32, (size, size), 0) >= lax.broadcasted_iota(
        jnp.int32, (size, size), 1
    )


def cumulative(decay):
    ones = jnp.where(lower(CHUNK), 1.0, 0.0).astype(BF16)
    high = decay.astype(BF16)
    rest = decay - high.astype(F32)
    mid = rest.astype(BF16)
    low = (rest - mid.astype(F32)).astype(BF16)
    return dot(ones, high) + dot(ones, mid) + dot(ones, low)


def split(x):
    high = x.astype(BF16)
    return jnp.concatenate([high, (x - high.astype(F32)).astype(BF16)], axis=1)


def spread(group, heads, columns):
    head = lax.broadcasted_iota(jnp.int32, (2 * heads, columns), 0)
    head = jnp.where(head >= heads, head - heads, head)
    column = lax.broadcasted_iota(jnp.int32, (2 * heads, columns), 1)
    first = (head - group * (columns // HEAD_DIM)) * HEAD_DIM
    return jnp.where((column >= first) & (column < first + HEAD_DIM), 1.0, 0.0).astype(BF16)


def factors(step_ref, decay_ref):
    half = CHUNK // 2 - 1
    out = []
    for c in range(2):
        rows = pl.ds(c * CHUNK, CHUNK)
        cum = cumulative(decay_ref[rows, :])
        mid, end = cum[half : half + 1], cum[CHUNK - 1 : CHUNK]
        out.append((step_ref[rows, :] * jnp.exp(mid - cum), jnp.exp(cum - mid), mid, end))
    return out


def pad8(rows):
    rows = list(rows)
    return jnp.concatenate(rows + [jnp.zeros_like(rows[0])] * (16 - len(rows)), axis=0)


def mixer_kernel(
    ways,
    seqs,
    x_hbm,
    step_hbm,
    decay_hbm,
    inject_hbm,
    readout_hbm,
    skip_ref,
    out_ref,
    x_ref,
    step_ref,
    decay_ref,
    inject_ref,
    readout_ref,
    held_ref,
    drive_ref,
    first_state,
    after_ref,
    left_ref,
    fac,
    fac_out,
    tot,
    pair,
    dec,
    up_stage,
    parts,
    down_stage,
    total_stage,
    total_in,
    next_stage,
    enter_in,
    tot_send,
    tot_recv,
    pair_send,
    pair_recv,
    up_send,
    up_recv,
    down_send,
    down_recv,
    total_send,
    total_recv,
    next_send,
    enter_recv,
    keep_sem,
    load_sem,
    x_sem,
):
    heads = step_ref.shape[1]
    width = x_ref.shape[1]
    own = width // ways
    depth = own // PIECE
    me, seq = lax.axis_index("head"), lax.axis_index("seq")
    core, chip = lax.rem(seq, 2), seq // 2
    chips = seqs // 2
    first = chip == 0

    def peer(q):
        return (seq, q)

    def other(i):
        return lax.rem(me + i, ways)

    def remote(src, dst, send, recv, device):
        return pltpu.make_async_remote_copy(
            src_ref=src,
            dst_ref=dst,
            send_sem=send,
            recv_sem=recv,
            device_id=device,
            device_id_type=MESH,
        )

    def load(i):
        src = (decay_hbm, step_hbm, inject_hbm, readout_hbm)[i]
        dst = (decay_ref, step_ref, inject_ref, readout_ref)[i]
        return pltpu.make_async_copy(src, dst, load_sem.at[i])

    def columns_of(index):
        return pl.ds(pl.multiple_of(index * PIECE, PIECE), PIECE)

    def load_x(index):
        columns = columns_of(index)
        return pltpu.make_async_copy(x_hbm.at[:, columns], x_ref.at[:, columns], x_sem.at[index])

    def place(t):
        return lax.rem(me + 1 + lax.rem(t, ways), ways) * depth + t // ways

    for i in range(3):
        load(i).start()

    def begin(t, carry):
        load_x(place(t)).start()
        return carry

    lax.fori_loop(0, depth * ways, begin, 0)
    load(3).start()

    barrier = pltpu.get_barrier_semaphore()

    def greet(device):
        pl.semaphore_signal(barrier, inc=1, device_id=device, device_id_type=MESH)

    for i in range(1, ways):
        greet(peer(other(i)))

    @pl.when(core == 1)
    def _():
        greet((seq - 1, me))

    @pl.when((core == 1) & (chip > 0))
    def _():
        greet((seq - 2, me))

    @pl.when((core == 0) & (chip > 0))
    def _():
        greet((seq - 1, me))

    load(0).wait()
    load(1).wait()
    (u0, w0, m0, e0), (u1, w1, m1, e1) = factors(step_ref, decay_ref)
    fac[...] = split(
        jnp.concatenate([u0, u1, pad8([jnp.exp(e0 - m0 + e1), jnp.exp(e1 - m1)])], axis=0)
    )
    aux = [jnp.exp(m0), jnp.exp(m1 + e0), jnp.exp(m1 + e0 - m0), skip_ref[...]]
    fac_out[...] = split(jnp.concatenate([w0, w1, pad8(aux)], axis=0))
    tot[me] = jnp.broadcast_to(e0 + e1, (8, heads))

    @pl.when(first)
    def _():
        enter_in[...] = jnp.zeros_like(enter_in)

    ahead = 2 - 2 * (chip // (chips - 1)) if chips > 1 else 0
    pl.semaphore_wait(barrier, ways - core + core * ahead)

    def tot_copy(q):
        return remote(tot.at[me], tot.at[me], tot_send.at[q], tot_recv.at[me], peer(q))

    def tot_from(q):
        return remote(tot.at[q], tot.at[q], tot_send.at[q], tot_recv.at[q], peer(q))

    def up_copy(k, q):
        return remote(
            up_stage.at[k, q], parts.at[k, me], up_send.at[k, q], up_recv.at[k, me], peer(q)
        )

    def up_from(k, q):
        return remote(
            up_stage.at[k, q], parts.at[k, q], up_send.at[k, q], up_recv.at[k, q], peer(q)
        )

    def down_copy(k, q):
        return remote(
            down_stage.at[k, q],
            held_ref.at[me * depth + k],
            down_send.at[k, q],
            down_recv.at[k, me],
            peer(q),
        )

    def down_from(k, q):
        return remote(
            down_stage.at[k, q],
            held_ref.at[q * depth + k],
            down_send.at[k, q],
            down_recv.at[k, q],
            peer(q),
        )

    def keep_copy(k):
        return pltpu.make_async_copy(
            down_stage.at[k, me], held_ref.at[me * depth + k], keep_sem.at[k]
        )

    def pair_copy():
        return remote(pair.at[0], pair.at[1], pair_send, pair_recv, (seq + 1, me))

    def total_copy(k):
        return remote(
            total_stage.at[k], total_in.at[k], total_send.at[k], total_recv.at[k], (seq + 1, me)
        )

    def next_copy(k, ahead):
        return remote(
            next_stage.at[k],
            enter_in.at[k],
            next_send.at[k, ahead - 1],
            enter_recv.at[k],
            (seq + ahead, me),
        )

    for i in range(1, ways):
        tot_copy(other(i)).start()

    def piece(t, carry):
        k, i = t // ways, lax.rem(t, ways)
        q = lax.rem(me + 1 + i, ways)
        index = q * depth + k
        columns = columns_of(index)
        group = index * PIECE // (width // GROUPS)
        shared = pl.ds(pl.multiple_of(group * STATE, STATE), STATE)
        load_x(index).wait()
        wide = dot(fac[...], spread(index, heads, PIECE))
        state = None
        for c in range(2):
            rows = slice(c * CHUNK, (c + 1) * CHUNK)
            drive = (wide[rows] * x_ref[rows, columns].astype(F32)).astype(BF16)
            drive_ref[rows, columns] = drive
            part = dot_rows(inject_ref[rows, shared], drive)
            if c == 0:
                first_state[index] = part
            part = part * wide[2 * CHUNK + c : 2 * CHUNK + c + 1]
            state = part if state is None else state + part

        @pl.when(i == ways - 1)
        def _():
            parts[k, me] = state.astype(BF16)

        @pl.when(i < ways - 1)
        def _():
            up_stage[k, q] = state.astype(BF16)
            up_copy(k, q).start()

        return carry

    load(2).wait()
    lax.fori_loop(0, depth * ways, piece, 0)

    for i in range(1, ways):
        tot_from(other(i)).wait_recv()
    logs = [tot[j][:1] for j in range(ways)]
    whole = sum(logs[1:], logs[0])

    @pl.when(core == 0)
    def _():
        pair[0] = jnp.broadcast_to(whole, (8, heads))
        pair_copy().start()
        pair[1] = jnp.zeros((8, heads), F32)

    @pl.when(core == 1)
    def _():
        pair_copy().wait_recv()

    rows = [jnp.exp(a) for a in logs] + [jnp.exp(pair[1][:1])]
    rows = split(jnp.concatenate(rows + [jnp.zeros_like(rows[0])] * (-len(rows) % 16), axis=0))
    for k in range(depth):
        dec[k] = dot(rows, spread(me * depth + k, heads, PIECE))

    def await_parts(k):
        for i in range(1, ways):
            up_from(k, other(i)).wait_recv()

    def onward(k, running, j):
        return running * dec[k, j : j + 1, :] + parts[k, j].astype(F32)

    def returns(k, running):
        for j in range(ways):
            down_stage[k, j] = running.astype(BF16)
            running = onward(k, running, j)
        return running

    def send_down(k):
        for i in range(1, ways):
            down_copy(k, other(i)).start()
        keep_copy(k).start()

    def await_enter(k):
        @pl.when(chip > 0)
        def _():
            next_copy(k, 1).wait_recv()

    @pl.when(core == 0)
    def _():
        def totals(k, carry):
            await_parts(k)
            running = parts[k, 0].astype(F32)
            for j in range(1, ways):
                running = onward(k, running, j)
            total_stage[k] = running.astype(BF16)
            total_copy(k).start()
            await_enter(k)
            returns(k, enter_in[k].astype(F32))
            send_down(k)
            return carry

        lax.fori_loop(0, depth, totals, 0)

    @pl.when(core == 1)
    def _():
        def finish(k, carry):
            await_parts(k)
            total_copy(k).wait_recv()
            await_enter(k)
            start = enter_in[k].astype(F32) * dec[k, ways : ways + 1, :]
            running = returns(k, start + total_in[k].astype(F32))

            @pl.when(chip < chips - 1)
            def _():
                next_stage[k] = running.astype(BF16)
                next_copy(k, 2).start()
                next_copy(k, 1).start()

            send_down(k)
            return carry

        lax.fori_loop(0, depth, finish, 0)

    load(3).wait()
    mask = lower(CHUNK)

    def prepare(index, carry):
        columns = columns_of(index)
        after_ref[:, columns] = dot(fac_out[...], spread(index, heads, PIECE))
        return carry

    def cross(group, carry):
        shared = pl.ds(pl.multiple_of(group * STATE, STATE), STATE)
        for c in range(2):
            rows = slice(c * CHUNK, (c + 1) * CHUNK)
            readout = readout_ref[rows, shared]
            both = dot_last(readout, inject_ref[rows, shared])
            left_ref[group, rows, :CHUNK] = jnp.where(mask, both, 0.0).astype(BF16)
            left_ref[group, rows, CHUNK:] = readout
        return carry

    lax.fori_loop(0, GROUPS, cross, 0)
    lax.fori_loop(0, width // PIECE, prepare, 0)

    def result(k, q):
        index = q * depth + k
        columns = columns_of(index)
        group = index * PIECE // (width // GROUPS)
        held = held_ref[index].astype(F32)
        rest = after_ref[2 * CHUNK : 2 * CHUNK + 8, columns]
        enter = held * rest[0:1]
        for c in range(2):
            rows = slice(c * CHUNK, (c + 1) * CHUNK)
            right = jnp.concatenate([drive_ref[rows, columns], enter.astype(BF16)], axis=0)
            acc = dot(left_ref[group, rows, :], right)
            plain = rest[3:4] * x_ref[rows, columns].astype(F32)
            out_ref[rows, columns] = (after_ref[rows, columns] * acc + plain).astype(BF16)
            if c == 0:
                enter = held * rest[1:2] + first_state[index] * rest[2:3]

    def results(t, carry):
        k, i = t // ways, lax.rem(t, ways)
        q = lax.rem(me + i, ways)

        @pl.when(i == 0)
        def _():
            keep_copy(k).wait()

        @pl.when(i > 0)
        def _():
            down_from(k, q).wait_recv()

        result(k, q)
        return carry

    lax.fori_loop(0, depth * ways, results, 0)

    def drain(k, carry):
        for i in range(1, ways):
            up_copy(k, other(i)).wait_send()
            down_copy(k, other(i)).wait_send()

        @pl.when(core == 0)
        def _():
            total_copy(k).wait_send()

        @pl.when((core == 1) & (chip < chips - 1))
        def _():
            next_copy(k, 2).wait_send()
            next_copy(k, 1).wait_send()

        return carry

    lax.fori_loop(0, depth, drain, 0)
    for i in range(1, ways):
        tot_copy(other(i)).wait_send()

    @pl.when(core == 0)
    def _():
        pair_copy().wait_send()


def shards(features, step_size, log_decay, inject, readout, skip_gain):
    ways, seqs = lax.axis_size("head"), lax.axis_size("seq")
    tokens, width = features.shape
    heads = step_size.shape[1]
    depth = width // ways // PIECE
    pieces = width // PIECE
    vmem = pl.BlockSpec(memory_space=pltpu.VMEM)
    dma = pltpu.SemaphoreType.DMA
    return pl.pallas_call(
        functools.partial(mixer_kernel, ways, seqs),
        in_specs=[pl.BlockSpec(memory_space=pltpu.HBM)] * 5 + [vmem],
        out_specs=vmem,
        out_shape=pltpu.VMEM((tokens, width), BF16),
        scratch_shapes=[
            pltpu.VMEM((tokens, width), BF16),
            pltpu.VMEM((tokens, heads), F32),
            pltpu.VMEM((tokens, heads), F32),
            pltpu.VMEM((tokens, GROUPS * STATE), BF16),
            pltpu.VMEM((tokens, GROUPS * STATE), BF16),
            pltpu.VMEM((pieces, STATE, PIECE), BF16),
            pltpu.VMEM((tokens, width), BF16),
            pltpu.VMEM((pieces, STATE, PIECE), F32),
            pltpu.VMEM((tokens + 16, width), F32),
            pltpu.VMEM((GROUPS, tokens, CHUNK + STATE), BF16),
            pltpu.VMEM((2 * CHUNK + 16, 2 * heads), BF16),
            pltpu.VMEM((2 * CHUNK + 16, 2 * heads), BF16),
            pltpu.VMEM((ways, 8, heads), F32),
            pltpu.VMEM((2, 8, heads), F32),
            pltpu.VMEM((depth, (ways + 16) // 16 * 16, PIECE), F32),
            pltpu.VMEM((depth, ways, STATE, PIECE), BF16),
            pltpu.VMEM((depth, ways, STATE, PIECE), BF16),
            pltpu.VMEM((depth, ways, STATE, PIECE), BF16),
            pltpu.VMEM((depth, STATE, PIECE), BF16),
            pltpu.VMEM((depth, STATE, PIECE), BF16),
            pltpu.VMEM((depth, STATE, PIECE), BF16),
            pltpu.VMEM((depth, STATE, PIECE), BF16),
            dma((ways,)),
            dma((ways,)),
            dma,
            dma,
            dma((depth, ways)),
            dma((depth, ways)),
            dma((depth, ways)),
            dma((depth, ways)),
            dma((depth,)),
            dma((depth,)),
            dma((depth, 2)),
            dma((depth,)),
            dma((depth,)),
            dma((4,)),
            dma((pieces,)),
        ],
        compiler_params=pltpu.CompilerParams(
            vmem_limit_bytes=59 * 2**20, collective_id=0, has_side_effects=True
        ),
    )(features, step_size, log_decay, inject, readout, skip_gain[None])


def solution(mesh):
    rows = P(("seq", "head"), None)
    return jax.shard_map(
        shards,
        mesh=mesh,
        in_specs=(rows, rows, rows, rows, rows, P()),
        out_specs=rows,
        check_vma=False,
    )
```

```python
import functools

import jax
import jax.numpy as jnp
from jax import lax
from jax.experimental import pallas as pl
from jax.experimental.pallas import tpu as pltpu
from jax.sharding import PartitionSpec as P

HEAD_DIM = 64
STATE = 128
GROUPS = 8
CHUNK = 128
PIECE = 256
MESH = pl.DeviceIdType.MESH
F32 = jnp.float32
BF16 = jnp.bfloat16


def dot(a, b):
    return jnp.dot(a, b, preferred_element_type=F32)


def dot_rows(a, b):
    return lax.dot_general(a, b, (((0,), (0,)), ((), ())), preferred_element_type=F32)


def dot_last(a, b):
    return lax.dot_general(a, b, (((1,), (1,)), ((), ())), preferred_element_type=F32)


def lower(size):
    return lax.broadcasted_iota(jnp.int32, (size, size), 0) >= lax.broadcasted_iota(
        jnp.int32, (size, size), 1
    )


def cumulative(decay):
    ones = jnp.where(lower(CHUNK), 1.0, 0.0).astype(BF16)
    high = decay.astype(BF16)
    rest = decay - high.astype(F32)
    mid = rest.astype(BF16)
    low = (rest - mid.astype(F32)).astype(BF16)
    return dot(ones, high) + dot(ones, mid) + dot(ones, low)


def split(x):
    high = x.astype(BF16)
    return jnp.concatenate([high, (x - high.astype(F32)).astype(BF16)], axis=1)


def spread(group, heads, columns):
    head = lax.broadcasted_iota(jnp.int32, (2 * heads, columns), 0)
    head = jnp.where(head >= heads, head - heads, head)
    column = lax.broadcasted_iota(jnp.int32, (2 * heads, columns), 1)
    first = (head - group * (columns // HEAD_DIM)) * HEAD_DIM
    return jnp.where((column >= first) & (column < first + HEAD_DIM), 1.0, 0.0).astype(BF16)


def factors(step_ref, decay_ref):
    half = CHUNK // 2 - 1
    out = []
    for c in range(2):
        rows = pl.ds(c * CHUNK, CHUNK)
        cum = cumulative(decay_ref[rows, :])
        mid, end = cum[half : half + 1], cum[CHUNK - 1 : CHUNK]
        out.append((step_ref[rows, :] * jnp.exp(mid - cum), jnp.exp(cum - mid), mid, end))
    return out


def pad8(rows):
    rows = list(rows)
    return jnp.concatenate(rows + [jnp.zeros_like(rows[0])] * (16 - len(rows)), axis=0)


def mixer_kernel(ways, seqs, *refs):
    levels = ways.bit_length() - 1
    refs = list(refs)

    def take(count):
        out = refs[:count]
        del refs[:count]
        return out

    x_hbm, step_hbm, decay_hbm, inject_hbm, readout_hbm, skip_ref, out_ref = take(7)
    x_ref, step_ref, decay_ref, inject_ref, readout_ref = take(5)
    drive_ref, first_state, after_ref, left_ref, fac, fac_out, tot, pair, dec = take(9)
    level_total, level_in, down_stage = take(levels), take(levels), take(levels)
    enter_at = take(levels + 1)
    top_total, total_in, next_stage, enter_in = take(4)
    tot_send, tot_recv, pair_send, pair_recv, up_send, up_recv, down_send, down_recv = take(8)
    total_send, total_recv, next_send, enter_recv, load_sem, x_sem = take(6)
    heads = step_ref.shape[1]
    width = x_ref.shape[1]
    depth = width // ways // PIECE
    me, seq = lax.axis_index("head"), lax.axis_index("seq")
    core, chip = lax.rem(seq, 2), seq // 2
    chips = seqs // 2
    bits = [lax.rem(me // 2**l, 2) for l in range(levels)]
    mates = [me + 2**l * (1 - 2 * bits[l]) for l in range(levels)]
    count = [ways // 2**l for l in range(levels + 1)]
    starts = [0]
    for l in range(levels):
        starts.append(starts[l] + bits[l] * count[l + 1])

    def peer(q):
        return (seq, q)

    def other(i):
        return lax.rem(me + i, ways)

    def remote(src, dst, send, recv, device):
        return pltpu.make_async_remote_copy(
            src_ref=src,
            dst_ref=dst,
            send_sem=send,
            recv_sem=recv,
            device_id=device,
            device_id_type=MESH,
        )

    def load(i):
        src = (decay_hbm, step_hbm, inject_hbm, readout_hbm)[i]
        dst = (decay_ref, step_ref, inject_ref, readout_ref)[i]
        return pltpu.make_async_copy(src, dst, load_sem.at[i])

    def columns_of(index):
        return pl.ds(pl.multiple_of(index * PIECE, PIECE), PIECE)

    def load_x(index):
        columns = columns_of(index)
        return pltpu.make_async_copy(x_hbm.at[:, columns], x_ref.at[:, columns], x_sem.at[index])

    def owner(i):
        return lax.rem(i + (1 - bits[0]) * count[1], ways)

    for i in range(3):
        load(i).start()

    def begin(t, carry):
        load_x(owner(lax.rem(t, ways)) * depth + t // ways).start()
        return carry

    lax.fori_loop(0, depth * ways, begin, 0)
    load(3).start()

    barrier = pltpu.get_barrier_semaphore()

    def greet(device):
        pl.semaphore_signal(barrier, inc=1, device_id=device, device_id_type=MESH)

    for i in range(1, ways):
        greet(peer(other(i)))

    @pl.when(core == 1)
    def _():
        greet((seq - 1, me))

    @pl.when((core == 1) & (chip > 0))
    def _():
        greet((seq - 2, me))

    @pl.when((core == 0) & (chip > 0))
    def _():
        greet((seq - 1, me))

    load(0).wait()
    load(1).wait()
    (u0, w0, m0, e0), (u1, w1, m1, e1) = factors(step_ref, decay_ref)
    fac[...] = split(
        jnp.concatenate([u0, u1, pad8([jnp.exp(e0 - m0 + e1), jnp.exp(e1 - m1)])], axis=0)
    )
    aux = [jnp.exp(m0), jnp.exp(m1 + e0), jnp.exp(m1 + e0 - m0), skip_ref[...]]
    fac_out[...] = split(jnp.concatenate([w0, w1, pad8(aux)], axis=0))
    tot[me] = jnp.broadcast_to(e0 + e1, (8, heads))

    @pl.when(chip == 0)
    def _():
        enter_in[...] = jnp.zeros_like(enter_in)

    ahead = 2 - 2 * (chip // (chips - 1)) if chips > 1 else 0
    pl.semaphore_wait(barrier, ways - core + core * ahead)

    def tot_copy(q):
        return remote(tot.at[me], tot.at[me], tot_send.at[q], tot_recv.at[me], peer(q))

    def tot_from(q):
        return remote(tot.at[q], tot.at[q], tot_send.at[q], tot_recv.at[q], peer(q))

    def up_copy(l, k):
        half = count[l + 1]
        return remote(
            level_total[l].at[pl.ds(k * count[l] + (1 - bits[l]) * half, half)],
            level_in[l].at[pl.ds(k * half, half)],
            up_send.at[l, k],
            up_recv.at[l, k],
            peer(mates[l]),
        )

    def down_copy(l, k):
        half = count[l + 1]
        return remote(
            down_stage[l].at[pl.ds(k * half, half)],
            enter_at[l].at[pl.ds(k * count[l] + bits[l] * half, half)],
            down_send.at[l, k],
            down_recv.at[l, k],
            peer(mates[l]),
        )

    def down_from(l, k):
        half = count[l + 1]
        return remote(
            down_stage[l].at[pl.ds(k * half, half)],
            enter_at[l].at[pl.ds(k * count[l] + (1 - bits[l]) * half, half)],
            down_send.at[l, k],
            down_recv.at[l, k],
            peer(mates[l]),
        )

    def pair_copy():
        return remote(pair.at[0], pair.at[1], pair_send, pair_recv, (seq + 1, me))

    def total_copy(k):
        return remote(
            top_total.at[k], total_in.at[k], total_send.at[k], total_recv.at[k], (seq + 1, me)
        )

    def next_copy(k, ahead):
        return remote(
            next_stage.at[k],
            enter_in.at[k],
            next_send.at[k, ahead - 1],
            enter_recv.at[k],
            (seq + ahead, me),
        )

    for i in range(1, ways):
        tot_copy(other(i)).start()

    def piece(t, carry):
        k, i = t // ways, lax.rem(t, ways)
        q = owner(i)
        index = q * depth + k
        columns = columns_of(index)
        group = index * PIECE // (width // GROUPS)
        shared = pl.ds(pl.multiple_of(group * STATE, STATE), STATE)
        load_x(index).wait()
        wide = dot(fac[...], spread(index, heads, PIECE))
        state = None
        for c in range(2):
            rows = slice(c * CHUNK, (c + 1) * CHUNK)
            drive = (wide[rows] * x_ref[rows, columns].astype(F32)).astype(BF16)
            drive_ref[rows, columns] = drive
            part = dot_rows(inject_ref[rows, shared], drive)
            if c == 0:
                first_state[index] = part
            part = part * wide[2 * CHUNK + c : 2 * CHUNK + c + 1]
            state = part if state is None else state + part
        level_total[0][k * ways + q] = state.astype(BF16)

        @pl.when(i == count[1] - 1)
        def _():
            up_copy(0, k).start()

        return carry

    load(2).wait()
    lax.fori_loop(0, depth * ways, piece, 0)

    for i in range(1, ways):
        tot_from(other(i)).wait_recv()

    def log_sum(first, n):
        rows = [tot[first + i][:1] for i in range(n)]
        return sum(rows[1:], rows[0])

    whole = log_sum(0, ways)

    @pl.when(core == 0)
    def _():
        pair[0] = jnp.broadcast_to(whole, (8, heads))
        pair_copy().start()
        pair[1] = jnp.zeros((8, heads), F32)

    @pl.when(core == 1)
    def _():
        pair_copy().wait_recv()

    rows = []
    for l in range(levels):
        base = me // 2 ** (l + 1) * 2 ** (l + 1)
        rows += [log_sum(base, 2**l), log_sum(base + 2**l, 2**l)]
    rows = split(jnp.exp(pad8(rows + [whole, pair[1][:1]])))

    def widen(t, carry):
        k, i = t // count[1], lax.rem(t, count[1])
        dec[t] = dot(rows, spread((starts[1] + i) * depth + k, heads, PIECE))
        return carry

    lax.fori_loop(0, depth * count[1], widen, 0)

    def decay_row(l, k, i, row):
        at = k * count[1] + starts[l + 1] - starts[1] + i
        return dec[at][row : row + 1]

    def sides(l, k, i):
        half = count[l + 1]
        own = level_total[l][k * count[l] + bits[l] * half + i].astype(F32)
        came = level_in[l][k * half + i].astype(F32)
        return jnp.where(bits[l] == 0, own, came), jnp.where(bits[l] == 0, came, own)

    def up(l, k):
        up_copy(l, k).wait_recv()
        for i in range(count[l + 1]):
            left, right = sides(l, k, i)
            both = (left * decay_row(l, k, i, 2 * l + 1) + right).astype(BF16)
            if l + 1 < levels:
                level_total[l + 1][k * count[l + 1] + i] = both
            else:
                top_total[k] = both
        if l + 1 < levels:
            up_copy(l + 1, k).start()
        else:

            @pl.when(core == 0)
            def _():
                total_copy(k).start()

    def top(k):
        @pl.when(chip > 0)
        def _():
            next_copy(k, 1).wait_recv()

        @pl.when(core == 0)
        def _():
            enter_at[levels][k] = enter_in[k]

        @pl.when(core == 1)
        def _():
            total_copy(k).wait_recv()
            start = enter_in[k].astype(F32) * decay_row(levels - 1, k, 0, 2 * levels + 1)
            start = start + total_in[k].astype(F32)
            after = start * decay_row(levels - 1, k, 0, 2 * levels) + top_total[k].astype(F32)

            @pl.when(chip < chips - 1)
            def _():
                next_stage[k] = after.astype(BF16)
                next_copy(k, 2).start()
                next_copy(k, 1).start()

            enter_at[levels][k] = start.astype(BF16)

    def down(l, k):
        half = count[l + 1]
        if l + 1 < levels:
            down_from(l + 1, k).wait_recv()
        for i in range(half):
            enter = enter_at[l + 1][k * half + i].astype(F32)
            left, _ = sides(l, k, i)
            later = enter * decay_row(l, k, i, 2 * l) + left
            mine = jnp.where(bits[l] == 0, enter, later)
            theirs = jnp.where(bits[l] == 0, later, enter)
            down_stage[l][k * half + i] = theirs.astype(BF16)
            enter_at[l][k * count[l] + bits[l] * half + i] = mine.astype(BF16)
        down_copy(l, k).start()

    mask = lower(CHUNK)

    def prepare(index, carry):
        columns = columns_of(index)
        after_ref[:, columns] = dot(fac_out[...], spread(index, heads, PIECE))
        return carry

    def cross(group, carry):
        shared = pl.ds(pl.multiple_of(group * STATE, STATE), STATE)
        for c in range(2):
            rows = slice(c * CHUNK, (c + 1) * CHUNK)
            readout = readout_ref[rows, shared]
            both = dot_last(readout, inject_ref[rows, shared])
            left_ref[group, rows, :CHUNK] = jnp.where(mask, both, 0.0).astype(BF16)
            left_ref[group, rows, CHUNK:] = readout
        return carry

    def advance(t, carry):
        def stage(lag, work):
            @pl.when((t >= lag) & (t < depth + lag))
            def _():
                work(t - lag)

        for l in range(levels):
            stage(l, functools.partial(up, l))
        stage(levels, top)
        for n, l in enumerate(reversed(range(levels))):
            stage(levels + n, functools.partial(down, l))

        @pl.when(t < depth)
        def _():
            lax.fori_loop(t * ways, (t + 1) * ways, prepare, 0)

        return carry

    lax.fori_loop(0, depth + 2 * levels - 1, advance, 0)
    load(3).wait()
    lax.fori_loop(0, GROUPS, cross, 0)

    def results(t, carry):
        k, i = t // ways, lax.rem(t, ways)
        q = lax.rem(i + bits[0] * count[1], ways)

        @pl.when(i == count[1])
        def _():
            down_from(0, k).wait_recv()

        index = q * depth + k
        columns = columns_of(index)
        group = index * PIECE // (width // GROUPS)
        held = enter_at[0][k * ways + q].astype(F32)
        rest = after_ref[2 * CHUNK : 2 * CHUNK + 8, columns]
        enter = held * rest[0:1]
        for c in range(2):
            rows = slice(c * CHUNK, (c + 1) * CHUNK)
            right = jnp.concatenate([drive_ref[rows, columns], enter.astype(BF16)], axis=0)
            acc = dot(left_ref[group, rows, :], right)
            plain = rest[3:4] * x_ref[rows, columns].astype(F32)
            out_ref[rows, columns] = (after_ref[rows, columns] * acc + plain).astype(BF16)
            if c == 0:
                enter = held * rest[1:2] + first_state[index] * rest[2:3]
        return carry

    lax.fori_loop(0, depth * ways, results, 0)

    def drain(k, carry):
        for l in range(levels):
            up_copy(l, k).wait_send()
            down_copy(l, k).wait_send()

        @pl.when(core == 0)
        def _():
            total_copy(k).wait_send()

        @pl.when((core == 1) & (chip < chips - 1))
        def _():
            next_copy(k, 2).wait_send()
            next_copy(k, 1).wait_send()

        return carry

    lax.fori_loop(0, depth, drain, 0)
    for i in range(1, ways):
        tot_copy(other(i)).wait_send()

    @pl.when(core == 0)
    def _():
        pair_copy().wait_send()


def shards(features, step_size, log_decay, inject, readout, skip_gain):
    ways, seqs = lax.axis_size("head"), lax.axis_size("seq")
    tokens, width = features.shape
    heads = step_size.shape[1]
    depth = width // ways // PIECE
    pieces = width // PIECE
    levels = ways.bit_length() - 1

    def states(count):
        return pltpu.VMEM((count, STATE, PIECE), BF16)

    vmem = pl.BlockSpec(memory_space=pltpu.VMEM)
    dma = pltpu.SemaphoreType.DMA
    return pl.pallas_call(
        functools.partial(mixer_kernel, ways, seqs),
        in_specs=[pl.BlockSpec(memory_space=pltpu.HBM)] * 5 + [vmem],
        out_specs=vmem,
        out_shape=pltpu.VMEM((tokens, width), BF16),
        scratch_shapes=[
            pltpu.VMEM((tokens, width), BF16),
            pltpu.VMEM((tokens, heads), F32),
            pltpu.VMEM((tokens, heads), F32),
            pltpu.VMEM((tokens, GROUPS * STATE), BF16),
            pltpu.VMEM((tokens, GROUPS * STATE), BF16),
            pltpu.VMEM((tokens, width), BF16),
            pltpu.VMEM((pieces, STATE, PIECE), F32),
            pltpu.VMEM((tokens + 16, width), F32),
            pltpu.VMEM((GROUPS, tokens, CHUNK + STATE), BF16),
            pltpu.VMEM((2 * CHUNK + 16, 2 * heads), BF16),
            pltpu.VMEM((2 * CHUNK + 16, 2 * heads), BF16),
            pltpu.VMEM((ways, 8, heads), F32),
            pltpu.VMEM((2, 8, heads), F32),
            pltpu.VMEM((pieces // 2, 16, PIECE), F32),
            *[states(pieces // 2**l) for l in range(levels)],
            *[states(pieces // 2 ** (l + 1)) for l in range(levels)],
            *[states(pieces // 2 ** (l + 1)) for l in range(levels)],
            *[states(pieces // 2**l) for l in range(levels + 1)],
            *[states(depth)] * 4,
            dma((ways,)),
            dma((ways,)),
            dma,
            dma,
            *[dma((levels, depth))] * 4,
            dma((depth,)),
            dma((depth,)),
            dma((depth, 2)),
            dma((depth,)),
            dma((4,)),
            dma((pieces,)),
        ],
        compiler_params=pltpu.CompilerParams(
            vmem_limit_bytes=59 * 2**20, collective_id=0, has_side_effects=True
        ),
    )(features, step_size, log_decay, inject, readout, skip_gain[None])


def solution(mesh):
    rows = P(("seq", "head"), None)
    return jax.shard_map(
        shards,
        mesh=mesh,
        in_specs=(rows, rows, rows, rows, rows, P()),
        out_specs=rows,
        check_vma=False,
    )
```

```python
import functools

import jax
import jax.numpy as jnp
from jax import lax
from jax.experimental import pallas as pl
from jax.experimental.pallas import tpu as pltpu
from jax.sharding import PartitionSpec as P

HEAD_DIM = 64
STATE = 128
GROUPS = 8
CHUNK = 128
PIECE = 256
MESH = pl.DeviceIdType.MESH
F32 = jnp.float32
BF16 = jnp.bfloat16


def dot(a, b):
    return jnp.dot(a, b, preferred_element_type=F32)


def dot_rows(a, b):
    return lax.dot_general(a, b, (((0,), (0,)), ((), ())), preferred_element_type=F32)


def dot_last(a, b):
    return lax.dot_general(a, b, (((1,), (1,)), ((), ())), preferred_element_type=F32)


def lower(size):
    return lax.broadcasted_iota(jnp.int32, (size, size), 0) >= lax.broadcasted_iota(
        jnp.int32, (size, size), 1
    )


def cumulative(decay):
    ones = jnp.where(lower(CHUNK), 1.0, 0.0).astype(BF16)
    high = decay.astype(BF16)
    rest = decay - high.astype(F32)
    mid = rest.astype(BF16)
    low = (rest - mid.astype(F32)).astype(BF16)
    return dot(ones, high) + dot(ones, mid) + dot(ones, low)


def split(x):
    high = x.astype(BF16)
    return jnp.concatenate([high, (x - high.astype(F32)).astype(BF16)], axis=1)


def spread(group, heads, columns):
    head = lax.broadcasted_iota(jnp.int32, (2 * heads, columns), 0)
    head = jnp.where(head >= heads, head - heads, head)
    column = lax.broadcasted_iota(jnp.int32, (2 * heads, columns), 1)
    first = (head - group * (columns // HEAD_DIM)) * HEAD_DIM
    return jnp.where((column >= first) & (column < first + HEAD_DIM), 1.0, 0.0).astype(BF16)


def factors(step_ref, decay_ref):
    half = CHUNK // 2 - 1
    out = []
    for c in range(2):
        rows = pl.ds(c * CHUNK, CHUNK)
        cum = cumulative(decay_ref[rows, :])
        mid, end = cum[half : half + 1], cum[CHUNK - 1 : CHUNK]
        out.append((step_ref[rows, :] * jnp.exp(mid - cum), jnp.exp(cum - mid), mid, end))
    return out


def pad8(rows):
    rows = list(rows)
    return jnp.concatenate(rows + [jnp.zeros_like(rows[0])] * (16 - len(rows)), axis=0)


def mixer_kernel(ways, seqs, *refs):
    levels = ways.bit_length() - 1
    refs = list(refs)

    def take(count):
        out = refs[:count]
        del refs[:count]
        return out

    x_hbm, step_hbm, decay_hbm, inject_hbm, readout_hbm, skip_ref, out_ref = take(7)
    x_ref, step_ref, decay_ref, inject_ref, readout_ref = take(5)
    drive_ref, first_state, after_ref, left_ref, fac, fac_out, tot, pair, dec = take(9)
    level_total, level_in, down_stage = take(levels), take(levels), take(levels)
    enter_at = take(levels + 1)
    top_total, total_in, next_stage, enter_in = take(4)
    tot_send, tot_recv, pair_send, pair_recv, up_send, up_recv, down_send, down_recv = take(8)
    total_send, total_recv, next_send, enter_recv, load_sem, x_sem = take(6)
    heads = step_ref.shape[1]
    width = x_ref.shape[1]
    depth = width // ways // PIECE
    me, seq = lax.axis_index("head"), lax.axis_index("seq")
    core, chip = lax.rem(seq, 2), seq // 2
    chips = seqs // 2
    bits = [lax.rem(me // 2**l, 2) for l in range(levels)]
    mates = [me + 2**l * (1 - 2 * bits[l]) for l in range(levels)]
    count = [ways // 2**l for l in range(levels + 1)]
    starts = [0]
    for l in range(levels):
        starts.append(starts[l] + bits[l] * count[l + 1])

    def peer(q):
        return (seq, q)

    def other(i):
        return lax.rem(me + i, ways)

    def remote(src, dst, send, recv, device):
        return pltpu.make_async_remote_copy(
            src_ref=src,
            dst_ref=dst,
            send_sem=send,
            recv_sem=recv,
            device_id=device,
            device_id_type=MESH,
        )

    def load(i):
        src = (decay_hbm, step_hbm, inject_hbm, readout_hbm)[i]
        dst = (decay_ref, step_ref, inject_ref, readout_ref)[i]
        return pltpu.make_async_copy(src, dst, load_sem.at[i])

    def columns_of(index):
        return pl.ds(pl.multiple_of(index * PIECE, PIECE), PIECE)

    def load_x(index):
        columns = columns_of(index)
        return pltpu.make_async_copy(x_hbm.at[:, columns], x_ref.at[:, columns], x_sem.at[index])

    def owner(i):
        return lax.rem(i + (1 - bits[0]) * count[1], ways)

    for i in range(3):
        load(i).start()

    def begin(t, carry):
        load_x(owner(lax.rem(t, ways)) * depth + t // ways).start()
        return carry

    lax.fori_loop(0, depth * ways, begin, 0)
    load(3).start()

    barrier = pltpu.get_barrier_semaphore()

    def greet(device):
        pl.semaphore_signal(barrier, inc=1, device_id=device, device_id_type=MESH)

    for i in range(1, ways):
        greet(peer(other(i)))

    @pl.when(core == 1)
    def _():
        greet((seq - 1, me))

    @pl.when((core == 1) & (chip > 0))
    def _():
        greet((seq - 2, me))

    @pl.when((core == 0) & (chip > 0))
    def _():
        greet((seq - 1, me))

    load(0).wait()
    load(1).wait()
    (u0, w0, m0, e0), (u1, w1, m1, e1) = factors(step_ref, decay_ref)
    fac[...] = split(
        jnp.concatenate([u0, u1, pad8([jnp.exp(e0 - m0 + e1), jnp.exp(e1 - m1)])], axis=0)
    )
    aux = [jnp.exp(m0), jnp.exp(m1 + e0), jnp.exp(m1 + e0 - m0), skip_ref[...]]
    fac_out[...] = split(jnp.concatenate([w0, w1, pad8(aux)], axis=0))
    tot[me] = jnp.broadcast_to(e0 + e1, (8, heads))

    @pl.when(chip == 0)
    def _():
        enter_in[...] = jnp.zeros_like(enter_in)

    ahead = 2 - 2 * (chip // (chips - 1)) if chips > 1 else 0
    pl.semaphore_wait(barrier, ways - core + core * ahead)

    def tot_copy(q):
        return remote(tot.at[me], tot.at[me], tot_send.at[q], tot_recv.at[me], peer(q))

    def tot_from(q):
        return remote(tot.at[q], tot.at[q], tot_send.at[q], tot_recv.at[q], peer(q))

    def up_copy(l, k):
        half = count[l + 1]
        return remote(
            level_total[l].at[pl.ds(k * count[l] + (1 - bits[l]) * half, half)],
            level_in[l].at[pl.ds(k * half, half)],
            up_send.at[l, k],
            up_recv.at[l, k],
            peer(mates[l]),
        )

    def down_copy(l, k):
        half = count[l + 1]
        return remote(
            down_stage[l].at[pl.ds(k * half, half)],
            enter_at[l].at[pl.ds(k * count[l] + bits[l] * half, half)],
            down_send.at[l, k],
            down_recv.at[l, k],
            peer(mates[l]),
        )

    def down_from(l, k):
        half = count[l + 1]
        return remote(
            down_stage[l].at[pl.ds(k * half, half)],
            enter_at[l].at[pl.ds(k * count[l] + (1 - bits[l]) * half, half)],
            down_send.at[l, k],
            down_recv.at[l, k],
            peer(mates[l]),
        )

    def pair_copy():
        return remote(pair.at[0], pair.at[1], pair_send, pair_recv, (seq + 1, me))

    def total_copy(k):
        return remote(
            top_total.at[k], total_in.at[k], total_send.at[k], total_recv.at[k], (seq + 1, me)
        )

    def next_copy(k, ahead):
        return remote(
            next_stage.at[k],
            enter_in.at[k],
            next_send.at[k, ahead - 1],
            enter_recv.at[k],
            (seq + ahead, me),
        )

    for i in range(1, ways):
        tot_copy(other(i)).start()

    def piece(t, carry):
        k, i = t // ways, lax.rem(t, ways)
        q = owner(i)
        index = q * depth + k
        columns = columns_of(index)
        group = index * PIECE // (width // GROUPS)
        shared = pl.ds(pl.multiple_of(group * STATE, STATE), STATE)
        load_x(index).wait()
        wide = dot(fac[...], spread(index, heads, PIECE))
        state = None
        for c in range(2):
            rows = slice(c * CHUNK, (c + 1) * CHUNK)
            drive = (wide[rows] * x_ref[rows, columns].astype(F32)).astype(BF16)
            drive_ref[rows, columns] = drive
            part = dot_rows(inject_ref[rows, shared], drive)
            if c == 0:
                first_state[index] = part
            part = part * wide[2 * CHUNK + c : 2 * CHUNK + c + 1]
            state = part if state is None else state + part
        level_total[0][k * ways + q] = state.astype(BF16)

        @pl.when(i == count[1] - 1)
        def _():
            up_copy(0, k).start()

        return carry

    load(2).wait()
    lax.fori_loop(0, depth * ways, piece, 0)

    for i in range(1, ways):
        tot_from(other(i)).wait_recv()

    def log_sum(first, n):
        rows = [tot[first + i][:1] for i in range(n)]
        return sum(rows[1:], rows[0])

    whole = log_sum(0, ways)

    @pl.when(core == 0)
    def _():
        pair[0] = jnp.broadcast_to(whole, (8, heads))
        pair_copy().start()
        pair[1] = jnp.zeros((8, heads), F32)

    @pl.when(core == 1)
    def _():
        pair_copy().wait_recv()

    rows = []
    for l in range(levels):
        base = me // 2 ** (l + 1) * 2 ** (l + 1)
        rows += [log_sum(base, 2**l), log_sum(base + 2**l, 2**l)]
    rows = split(jnp.exp(pad8(rows + [whole, pair[1][:1]])))

    def widen(t, carry):
        k, i = t // count[1], lax.rem(t, count[1])
        dec[t] = dot(rows, spread((starts[1] + i) * depth + k, heads, PIECE))
        return carry

    lax.fori_loop(0, depth * count[1], widen, 0)

    def decay_row(l, k, i, row):
        at = k * count[1] + starts[l + 1] - starts[1] + i
        return dec[at][row : row + 1]

    def sides(l, k, i):
        half = count[l + 1]
        own = level_total[l][k * count[l] + bits[l] * half + i].astype(F32)
        came = level_in[l][k * half + i].astype(F32)
        return jnp.where(bits[l] == 0, own, came), jnp.where(bits[l] == 0, came, own)

    def up(l, k):
        up_copy(l, k).wait_recv()
        for i in range(count[l + 1]):
            left, right = sides(l, k, i)
            both = (left * decay_row(l, k, i, 2 * l + 1) + right).astype(BF16)
            if l + 1 < levels:
                level_total[l + 1][k * count[l + 1] + i] = both
            else:
                top_total[k] = both
        if l + 1 < levels:
            up_copy(l + 1, k).start()
        else:

            @pl.when(core == 0)
            def _():
                total_copy(k).start()

    def top(k):
        @pl.when(chip > 0)
        def _():
            next_copy(k, 1).wait_recv()

        @pl.when(core == 0)
        def _():
            enter_at[levels][k] = enter_in[k]

        @pl.when(core == 1)
        def _():
            total_copy(k).wait_recv()
            start = enter_in[k].astype(F32) * decay_row(levels - 1, k, 0, 2 * levels + 1)
            start = start + total_in[k].astype(F32)
            after = start * decay_row(levels - 1, k, 0, 2 * levels) + top_total[k].astype(F32)

            @pl.when(chip < chips - 1)
            def _():
                next_stage[k] = after.astype(BF16)
                next_copy(k, 2).start()
                next_copy(k, 1).start()

            enter_at[levels][k] = start.astype(BF16)

    def down(l, k):
        half = count[l + 1]
        if l + 1 < levels:
            down_from(l + 1, k).wait_recv()
        for i in range(half):
            enter = enter_at[l + 1][k * half + i].astype(F32)
            left, _ = sides(l, k, i)
            later = enter * decay_row(l, k, i, 2 * l) + left
            mine = jnp.where(bits[l] == 0, enter, later)
            theirs = jnp.where(bits[l] == 0, later, enter)
            down_stage[l][k * half + i] = theirs.astype(BF16)
            enter_at[l][k * count[l] + bits[l] * half + i] = mine.astype(BF16)
        down_copy(l, k).start()

    mask = lower(CHUNK)

    def prepare(index, carry):
        columns = columns_of(index)
        after_ref[:, columns] = dot(fac_out[...], spread(index, heads, PIECE))
        return carry

    def cross(group, carry):
        shared = pl.ds(pl.multiple_of(group * STATE, STATE), STATE)
        for c in range(2):
            rows = slice(c * CHUNK, (c + 1) * CHUNK)
            readout = readout_ref[rows, shared]
            both = dot_last(readout, inject_ref[rows, shared])
            left_ref[group, rows, :CHUNK] = jnp.where(mask, both, 0.0).astype(BF16)
            left_ref[group, rows, CHUNK:] = readout
        return carry

    final_lag = max(depth, 2 * levels + chips - 2)

    def advance(t, carry):
        def stage(lag, work):
            @pl.when((t >= lag) & (t < depth + lag))
            def _():
                work(t - lag)

        for l in range(levels):
            stage(l, functools.partial(up, l))
        stage(levels + chip, top)
        for l in reversed(range(1, levels)):
            stage(levels + chip + levels - 1 - l, functools.partial(down, l))
        stage(final_lag, functools.partial(down, 0))

        @pl.when(t < depth)
        def _():
            lax.fori_loop(t * ways, (t + 1) * ways, prepare, 0)

        return carry

    lax.fori_loop(0, depth + final_lag, advance, 0)
    load(3).wait()
    lax.fori_loop(0, GROUPS, cross, 0)

    def results(t, carry):
        k, i = t // ways, lax.rem(t, ways)
        q = lax.rem(i + bits[0] * count[1], ways)

        @pl.when(i == count[1])
        def _():
            down_from(0, k).wait_recv()

        index = q * depth + k
        columns = columns_of(index)
        group = index * PIECE // (width // GROUPS)
        held = enter_at[0][k * ways + q].astype(F32)
        rest = after_ref[2 * CHUNK : 2 * CHUNK + 8, columns]
        enter = held * rest[0:1]
        for c in range(2):
            rows = slice(c * CHUNK, (c + 1) * CHUNK)
            right = jnp.concatenate([drive_ref[rows, columns], enter.astype(BF16)], axis=0)
            acc = dot(left_ref[group, rows, :], right)
            plain = rest[3:4] * x_ref[rows, columns].astype(F32)
            out_ref[rows, columns] = (after_ref[rows, columns] * acc + plain).astype(BF16)
            if c == 0:
                enter = held * rest[1:2] + first_state[index] * rest[2:3]
        return carry

    lax.fori_loop(0, depth * ways, results, 0)

    def drain(k, carry):
        for l in range(levels):
            up_copy(l, k).wait_send()
            down_copy(l, k).wait_send()

        @pl.when(core == 0)
        def _():
            total_copy(k).wait_send()

        @pl.when((core == 1) & (chip < chips - 1))
        def _():
            next_copy(k, 2).wait_send()
            next_copy(k, 1).wait_send()

        return carry

    lax.fori_loop(0, depth, drain, 0)
    for i in range(1, ways):
        tot_copy(other(i)).wait_send()

    @pl.when(core == 0)
    def _():
        pair_copy().wait_send()


def shards(features, step_size, log_decay, inject, readout, skip_gain):
    ways, seqs = lax.axis_size("head"), lax.axis_size("seq")
    tokens, width = features.shape
    heads = step_size.shape[1]
    depth = width // ways // PIECE
    pieces = width // PIECE
    levels = ways.bit_length() - 1

    def states(count):
        return pltpu.VMEM((count, STATE, PIECE), BF16)

    vmem = pl.BlockSpec(memory_space=pltpu.VMEM)
    dma = pltpu.SemaphoreType.DMA
    return pl.pallas_call(
        functools.partial(mixer_kernel, ways, seqs),
        in_specs=[pl.BlockSpec(memory_space=pltpu.HBM)] * 5 + [vmem],
        out_specs=vmem,
        out_shape=pltpu.VMEM((tokens, width), BF16),
        scratch_shapes=[
            pltpu.VMEM((tokens, width), BF16),
            pltpu.VMEM((tokens, heads), F32),
            pltpu.VMEM((tokens, heads), F32),
            pltpu.VMEM((tokens, GROUPS * STATE), BF16),
            pltpu.VMEM((tokens, GROUPS * STATE), BF16),
            pltpu.VMEM((tokens, width), BF16),
            pltpu.VMEM((pieces, STATE, PIECE), F32),
            pltpu.VMEM((tokens + 16, width), F32),
            pltpu.VMEM((GROUPS, tokens, CHUNK + STATE), BF16),
            pltpu.VMEM((2 * CHUNK + 16, 2 * heads), BF16),
            pltpu.VMEM((2 * CHUNK + 16, 2 * heads), BF16),
            pltpu.VMEM((ways, 8, heads), F32),
            pltpu.VMEM((2, 8, heads), F32),
            pltpu.VMEM((pieces // 2, 16, PIECE), F32),
            *[states(pieces // 2**l) for l in range(levels)],
            *[states(pieces // 2 ** (l + 1)) for l in range(levels)],
            *[states(pieces // 2 ** (l + 1)) for l in range(levels)],
            *[states(pieces // 2**l) for l in range(levels + 1)],
            *[states(depth)] * 4,
            dma((ways,)),
            dma((ways,)),
            dma,
            dma,
            *[dma((levels, depth))] * 4,
            dma((depth,)),
            dma((depth,)),
            dma((depth, 2)),
            dma((depth,)),
            dma((4,)),
            dma((pieces,)),
        ],
        compiler_params=pltpu.CompilerParams(
            vmem_limit_bytes=59 * 2**20, collective_id=0, has_side_effects=True
        ),
    )(features, step_size, log_decay, inject, readout, skip_gain[None])


def solution(mesh):
    rows = P(("seq", "head"), None)
    return jax.shard_map(
        shards,
        mesh=mesh,
        in_specs=(rows, rows, rows, rows, rows, P()),
        out_specs=rows,
        check_vma=False,
    )
```

```python
import functools

import jax
import jax.numpy as jnp
from jax import lax
from jax.experimental import pallas as pl
from jax.experimental.pallas import tpu as pltpu
from jax.sharding import PartitionSpec as P

HEAD_DIM = 64
STATE = 128
GROUPS = 8
CHUNK = 128
PIECE = 512
BEHIND = 2
MESH = pl.DeviceIdType.MESH
F32 = jnp.float32
BF16 = jnp.bfloat16


def dot(a, b):
    return jnp.dot(a, b, preferred_element_type=F32)


def dot_rows(a, b):
    return lax.dot_general(a, b, (((0,), (0,)), ((), ())), preferred_element_type=F32)


def dot_last(a, b):
    return lax.dot_general(a, b, (((1,), (1,)), ((), ())), preferred_element_type=F32)


def lower(size):
    return lax.broadcasted_iota(jnp.int32, (size, size), 0) >= lax.broadcasted_iota(
        jnp.int32, (size, size), 1
    )


def cumulative(decay):
    ones = jnp.where(lower(CHUNK), 1.0, 0.0).astype(BF16)
    high = decay.astype(BF16)
    rest = decay - high.astype(F32)
    mid = rest.astype(BF16)
    low = (rest - mid.astype(F32)).astype(BF16)
    return dot(ones, high) + dot(ones, mid) + dot(ones, low)


def split(x):
    high = x.astype(BF16)
    return jnp.concatenate([high, (x - high.astype(F32)).astype(BF16)], axis=1)


def spread(group, heads, columns):
    head = lax.broadcasted_iota(jnp.int32, (2 * heads, columns), 0)
    head = jnp.where(head >= heads, head - heads, head)
    column = lax.broadcasted_iota(jnp.int32, (2 * heads, columns), 1)
    first = (head - group * (columns // HEAD_DIM)) * HEAD_DIM
    return jnp.where((column >= first) & (column < first + HEAD_DIM), 1.0, 0.0).astype(BF16)


def factors(step_ref, decay_ref):
    half = CHUNK // 2 - 1
    out = []
    for c in range(2):
        rows = pl.ds(c * CHUNK, CHUNK)
        cum = cumulative(decay_ref[rows, :])
        mid, end = cum[half : half + 1], cum[CHUNK - 1 : CHUNK]
        out.append((step_ref[rows, :] * jnp.exp(mid - cum), jnp.exp(cum - mid), mid, end))
    return out


def pad8(rows):
    rows = list(rows)
    return jnp.concatenate(rows + [jnp.zeros_like(rows[0])] * (16 - len(rows)), axis=0)


def mixer_kernel(
    ways,
    seqs,
    x_hbm,
    step_hbm,
    decay_hbm,
    inject_hbm,
    readout_hbm,
    skip_ref,
    out_ref,
    x_ref,
    step_ref,
    decay_ref,
    inject_ref,
    readout_ref,
    held_ref,
    drive_ref,
    first_state,
    after_ref,
    left_ref,
    fac,
    fac_out,
    tot,
    pair,
    dec,
    up_stage,
    parts,
    down_stage,
    total_stage,
    total_in,
    next_stage,
    enter_in,
    tot_send,
    tot_recv,
    pair_send,
    pair_recv,
    up_send,
    up_recv,
    down_send,
    down_recv,
    total_send,
    total_recv,
    next_send,
    enter_recv,
    keep_sem,
    load_sem,
    x_sem,
):
    heads = step_ref.shape[1]
    width = x_ref.shape[1]
    own = width // ways
    depth = own // PIECE
    me, seq = lax.axis_index("head"), lax.axis_index("seq")
    core, chip = lax.rem(seq, 2), seq // 2
    chips = seqs // 2
    first = chip == 0

    def peer(q):
        return (seq, q)

    def other(i):
        return lax.rem(me + i, ways)

    def remote(src, dst, send, recv, device):
        return pltpu.make_async_remote_copy(
            src_ref=src,
            dst_ref=dst,
            send_sem=send,
            recv_sem=recv,
            device_id=device,
            device_id_type=MESH,
        )

    def load(i):
        src = (decay_hbm, step_hbm, inject_hbm, readout_hbm)[i]
        dst = (decay_ref, step_ref, inject_ref, readout_ref)[i]
        return pltpu.make_async_copy(src, dst, load_sem.at[i])

    def columns_of(index):
        return pl.ds(pl.multiple_of(index * PIECE, PIECE), PIECE)

    def load_x(index):
        columns = columns_of(index)
        return pltpu.make_async_copy(x_hbm.at[:, columns], x_ref.at[:, columns], x_sem.at[index])

    def place(t):
        return lax.rem(me + 1 + lax.rem(t, ways), ways) * depth + t // ways

    for i in range(3):
        load(i).start()

    def begin(t, carry):
        load_x(place(t)).start()
        return carry

    lax.fori_loop(0, depth * ways, begin, 0)
    load(3).start()

    barrier = pltpu.get_barrier_semaphore()

    def greet(device):
        pl.semaphore_signal(barrier, inc=1, device_id=device, device_id_type=MESH)

    for i in range(1, ways):
        greet(peer(other(i)))

    @pl.when(core == 1)
    def _():
        greet((seq - 1, me))

    @pl.when((core == 1) & (chip > 0))
    def _():
        greet((seq - 2, me))

    @pl.when((core == 0) & (chip > 0))
    def _():
        greet((seq - 1, me))

    load(0).wait()
    load(1).wait()
    (u0, w0, m0, e0), (u1, w1, m1, e1) = factors(step_ref, decay_ref)
    fac[...] = split(
        jnp.concatenate([u0, u1, pad8([jnp.exp(e0 - m0 + e1), jnp.exp(e1 - m1)])], axis=0)
    )
    aux = [jnp.exp(m0), jnp.exp(m1 + e0), jnp.exp(m1 + e0 - m0), skip_ref[...]]
    fac_out[...] = split(jnp.concatenate([w0, w1, pad8(aux)], axis=0))
    tot[me] = jnp.broadcast_to(e0 + e1, (8, heads))

    @pl.when(first)
    def _():
        enter_in[...] = jnp.zeros_like(enter_in)

    ahead = 2 - 2 * (chip // (chips - 1)) if chips > 1 else 0
    pl.semaphore_wait(barrier, ways - core + core * ahead)

    def tot_copy(q):
        return remote(tot.at[me], tot.at[me], tot_send.at[q], tot_recv.at[me], peer(q))

    def tot_from(q):
        return remote(tot.at[q], tot.at[q], tot_send.at[q], tot_recv.at[q], peer(q))

    def up_copy(k, q):
        return remote(
            up_stage.at[k, q], parts.at[k, me], up_send.at[k, q], up_recv.at[k, me], peer(q)
        )

    def up_from(k, q):
        return remote(
            up_stage.at[k, q], parts.at[k, q], up_send.at[k, q], up_recv.at[k, q], peer(q)
        )

    def down_copy(k, q):
        return remote(
            down_stage.at[k, q],
            held_ref.at[me * depth + k],
            down_send.at[k, q],
            down_recv.at[k, me],
            peer(q),
        )

    def down_from(k, q):
        return remote(
            down_stage.at[k, q],
            held_ref.at[q * depth + k],
            down_send.at[k, q],
            down_recv.at[k, q],
            peer(q),
        )

    def keep_copy(k):
        return pltpu.make_async_copy(
            down_stage.at[k, me], held_ref.at[me * depth + k], keep_sem.at[k]
        )

    def pair_copy():
        return remote(pair.at[0], pair.at[1], pair_send, pair_recv, (seq + 1, me))

    def total_copy(k):
        return remote(
            total_stage.at[k], total_in.at[k], total_send.at[k], total_recv.at[k], (seq + 1, me)
        )

    def next_copy(k, ahead):
        return remote(
            next_stage.at[k],
            enter_in.at[k],
            next_send.at[k, ahead - 1],
            enter_recv.at[k],
            (seq + ahead, me),
        )

    for i in range(1, ways):
        tot_copy(other(i)).start()

    def piece(t, carry):
        k, i = t // ways, lax.rem(t, ways)
        q = lax.rem(me + 1 + i, ways)
        index = q * depth + k
        columns = columns_of(index)
        group = index * PIECE // (width // GROUPS)
        shared = pl.ds(pl.multiple_of(group * STATE, STATE), STATE)
        load_x(index).wait()
        wide = dot(fac[...], spread(index, heads, PIECE))
        state = None
        for c in range(2):
            rows = slice(c * CHUNK, (c + 1) * CHUNK)
            drive = (wide[rows] * x_ref[rows, columns].astype(F32)).astype(BF16)
            drive_ref[rows, columns] = drive
            part = dot_rows(inject_ref[rows, shared], drive)
            if c == 0:
                first_state[index] = part
            part = part * wide[2 * CHUNK + c : 2 * CHUNK + c + 1]
            state = part if state is None else state + part

        @pl.when(i == ways - 1)
        def _():
            parts[k, me] = state.astype(BF16)

        @pl.when(i < ways - 1)
        def _():
            up_stage[k, q] = state.astype(BF16)
            up_copy(k, q).start()

        return carry

    load(2).wait()
    lax.fori_loop(0, depth * ways, piece, 0)

    for i in range(1, ways):
        tot_from(other(i)).wait_recv()
    logs = [tot[j][:1] for j in range(ways)]
    whole = sum(logs[1:], logs[0])

    @pl.when(core == 0)
    def _():
        pair[0] = jnp.broadcast_to(whole, (8, heads))
        pair_copy().start()
        pair[1] = jnp.zeros((8, heads), F32)

    @pl.when(core == 1)
    def _():
        pair_copy().wait_recv()

    rows = [jnp.exp(a) for a in logs] + [jnp.exp(pair[1][:1])]
    rows = split(jnp.concatenate(rows + [jnp.zeros_like(rows[0])] * (-len(rows) % 16), axis=0))
    for k in range(depth):
        dec[k] = dot(rows, spread(me * depth + k, heads, PIECE))

    def await_parts(k):
        for i in range(1, ways):
            up_from(k, other(i)).wait_recv()

    def onward(k, running, j):
        return running * dec[k, j : j + 1, :] + parts[k, j].astype(F32)

    def returns(k, running):
        for j in range(ways):
            down_stage[k, j] = running.astype(BF16)
            running = onward(k, running, j)
        return running

    def send_down(k):
        for i in range(1, ways):
            down_copy(k, other(i)).start()
        keep_copy(k).start()

    def await_enter(k):
        @pl.when(chip > 0)
        def _():
            next_copy(k, 1).wait_recv()

    @pl.when(core == 0)
    def _():
        def totals(k):
            await_parts(k)
            running = parts[k, 0].astype(F32)
            for j in range(1, ways):
                running = onward(k, running, j)
            total_stage[k] = running.astype(BF16)
            total_copy(k).start()

        def finish(k):
            await_enter(k)
            returns(k, enter_in[k].astype(F32))
            send_down(k)

        def both(t, carry):
            @pl.when(t < depth)
            def _():
                totals(t)

            @pl.when(t >= BEHIND)
            def _():
                finish(t - BEHIND)

            return carry

        lax.fori_loop(0, depth + BEHIND, both, 0)

    @pl.when(core == 1)
    def _():
        def finish(k, carry):
            await_parts(k)
            total_copy(k).wait_recv()
            await_enter(k)
            start = enter_in[k].astype(F32) * dec[k, ways : ways + 1, :]
            running = returns(k, start + total_in[k].astype(F32))

            @pl.when(chip < chips - 1)
            def _():
                next_stage[k] = running.astype(BF16)
                next_copy(k, 2).start()
                next_copy(k, 1).start()

            send_down(k)
            return carry

        lax.fori_loop(0, depth, finish, 0)

    load(3).wait()
    mask = lower(CHUNK)

    def prepare(index, carry):
        columns = columns_of(index)
        after_ref[:, columns] = dot(fac_out[...], spread(index, heads, PIECE))
        return carry

    def cross(group, carry):
        shared = pl.ds(pl.multiple_of(group * STATE, STATE), STATE)
        for c in range(2):
            rows = slice(c * CHUNK, (c + 1) * CHUNK)
            readout = readout_ref[rows, shared]
            both = dot_last(readout, inject_ref[rows, shared])
            left_ref[group, rows, :CHUNK] = jnp.where(mask, both, 0.0).astype(BF16)
            left_ref[group, rows, CHUNK:] = readout
        return carry

    lax.fori_loop(0, GROUPS, cross, 0)
    lax.fori_loop(0, width // PIECE, prepare, 0)

    def result(k, q):
        index = q * depth + k
        columns = columns_of(index)
        group = index * PIECE // (width // GROUPS)
        held = held_ref[index].astype(F32)
        rest = after_ref[2 * CHUNK : 2 * CHUNK + 8, columns]
        enter = held * rest[0:1]
        for c in range(2):
            rows = slice(c * CHUNK, (c + 1) * CHUNK)
            right = jnp.concatenate([drive_ref[rows, columns], enter.astype(BF16)], axis=0)
            acc = dot(left_ref[group, rows, :], right)
            plain = rest[3:4] * x_ref[rows, columns].astype(F32)
            out_ref[rows, columns] = (after_ref[rows, columns] * acc + plain).astype(BF16)
            if c == 0:
                enter = held * rest[1:2] + first_state[index] * rest[2:3]

    def results(t, carry):
        k, i = t // ways, lax.rem(t, ways)
        q = lax.rem(me + i, ways)

        @pl.when(i == 0)
        def _():
            keep_copy(k).wait()

        @pl.when(i > 0)
        def _():
            down_from(k, q).wait_recv()

        result(k, q)
        return carry

    lax.fori_loop(0, depth * ways, results, 0)

    def drain(k, carry):
        for i in range(1, ways):
            up_copy(k, other(i)).wait_send()
            down_copy(k, other(i)).wait_send()

        @pl.when(core == 0)
        def _():
            total_copy(k).wait_send()

        @pl.when((core == 1) & (chip < chips - 1))
        def _():
            next_copy(k, 2).wait_send()
            next_copy(k, 1).wait_send()

        return carry

    lax.fori_loop(0, depth, drain, 0)
    for i in range(1, ways):
        tot_copy(other(i)).wait_send()

    @pl.when(core == 0)
    def _():
        pair_copy().wait_send()


def shards(features, step_size, log_decay, inject, readout, skip_gain):
    ways, seqs = lax.axis_size("head"), lax.axis_size("seq")
    tokens, width = features.shape
    heads = step_size.shape[1]
    depth = width // ways // PIECE
    pieces = width // PIECE
    vmem = pl.BlockSpec(memory_space=pltpu.VMEM)
    dma = pltpu.SemaphoreType.DMA
    return pl.pallas_call(
        functools.partial(mixer_kernel, ways, seqs),
        in_specs=[pl.BlockSpec(memory_space=pltpu.HBM)] * 5 + [vmem],
        out_specs=vmem,
        out_shape=pltpu.VMEM((tokens, width), BF16),
        scratch_shapes=[
            pltpu.VMEM((tokens, width), BF16),
            pltpu.VMEM((tokens, heads), F32),
            pltpu.VMEM((tokens, heads), F32),
            pltpu.VMEM((tokens, GROUPS * STATE), BF16),
            pltpu.VMEM((tokens, GROUPS * STATE), BF16),
            pltpu.VMEM((pieces, STATE, PIECE), BF16),
            pltpu.VMEM((tokens, width), BF16),
            pltpu.VMEM((pieces, STATE, PIECE), F32),
            pltpu.VMEM((tokens + 16, width), F32),
            pltpu.VMEM((GROUPS, tokens, CHUNK + STATE), BF16),
            pltpu.VMEM((2 * CHUNK + 16, 2 * heads), BF16),
            pltpu.VMEM((2 * CHUNK + 16, 2 * heads), BF16),
            pltpu.VMEM((ways, 8, heads), F32),
            pltpu.VMEM((2, 8, heads), F32),
            pltpu.VMEM((depth, (ways + 16) // 16 * 16, PIECE), F32),
            pltpu.VMEM((depth, ways, STATE, PIECE), BF16),
            pltpu.VMEM((depth, ways, STATE, PIECE), BF16),
            pltpu.VMEM((depth, ways, STATE, PIECE), BF16),
            pltpu.VMEM((depth, STATE, PIECE), BF16),
            pltpu.VMEM((depth, STATE, PIECE), BF16),
            pltpu.VMEM((depth, STATE, PIECE), BF16),
            pltpu.VMEM((depth, STATE, PIECE), BF16),
            dma((ways,)),
            dma((ways,)),
            dma,
            dma,
            dma((depth, ways)),
            dma((depth, ways)),
            dma((depth, ways)),
            dma((depth, ways)),
            dma((depth,)),
            dma((depth,)),
            dma((depth, 2)),
            dma((depth,)),
            dma((depth,)),
            dma((4,)),
            dma((pieces,)),
        ],
        compiler_params=pltpu.CompilerParams(
            vmem_limit_bytes=59 * 2**20, collective_id=0, has_side_effects=True
        ),
    )(features, step_size, log_decay, inject, readout, skip_gain[None])


def solution(mesh):
    rows = P(("seq", "head"), None)
    return jax.shard_map(
        shards,
        mesh=mesh,
        in_specs=(rows, rows, rows, rows, rows, P()),
        out_specs=rows,
        check_vma=False,
    )
```

```python
import functools

import jax
import jax.numpy as jnp
from jax import lax
from jax.experimental import pallas as pl
from jax.experimental.pallas import tpu as pltpu
from jax.sharding import PartitionSpec as P

HEAD_DIM = 64
STATE = 128
GROUPS = 8
CHUNK = 128
PIECE = 512
BEHIND = 2
STORES = 8
MESH = pl.DeviceIdType.MESH
F32 = jnp.float32
BF16 = jnp.bfloat16


def dot(a, b):
    return jnp.dot(a, b, preferred_element_type=F32)


def dot_rows(a, b):
    return lax.dot_general(a, b, (((0,), (0,)), ((), ())), preferred_element_type=F32)


def dot_last(a, b):
    return lax.dot_general(a, b, (((1,), (1,)), ((), ())), preferred_element_type=F32)


def lower(size):
    return lax.broadcasted_iota(jnp.int32, (size, size), 0) >= lax.broadcasted_iota(
        jnp.int32, (size, size), 1
    )


def cumulative(decay):
    ones = jnp.where(lower(CHUNK), 1.0, 0.0).astype(BF16)
    high = decay.astype(BF16)
    rest = decay - high.astype(F32)
    mid = rest.astype(BF16)
    low = (rest - mid.astype(F32)).astype(BF16)
    return dot(ones, high) + dot(ones, mid) + dot(ones, low)


def split(x):
    high = x.astype(BF16)
    return jnp.concatenate([high, (x - high.astype(F32)).astype(BF16)], axis=1)


def spread(group, heads, columns):
    head = lax.broadcasted_iota(jnp.int32, (2 * heads, columns), 0)
    head = jnp.where(head >= heads, head - heads, head)
    column = lax.broadcasted_iota(jnp.int32, (2 * heads, columns), 1)
    first = (head - group * (columns // HEAD_DIM)) * HEAD_DIM
    return jnp.where((column >= first) & (column < first + HEAD_DIM), 1.0, 0.0).astype(BF16)


def factors(step_ref, decay_ref):
    half = CHUNK // 2 - 1
    out = []
    for c in range(2):
        rows = pl.ds(c * CHUNK, CHUNK)
        cum = cumulative(decay_ref[rows, :])
        mid, end = cum[half : half + 1], cum[CHUNK - 1 : CHUNK]
        out.append((step_ref[rows, :] * jnp.exp(mid - cum), jnp.exp(cum - mid), mid, end))
    return out


def pad8(rows):
    rows = list(rows)
    return jnp.concatenate(rows + [jnp.zeros_like(rows[0])] * (16 - len(rows)), axis=0)


def mixer_kernel(
    ways,
    seqs,
    x_hbm,
    step_hbm,
    decay_hbm,
    inject_hbm,
    readout_hbm,
    skip_ref,
    out_ref,
    x_ref,
    step_ref,
    decay_ref,
    inject_ref,
    readout_ref,
    held_ref,
    drive_ref,
    first_state,
    after_ref,
    left_ref,
    fac,
    fac_out,
    tot,
    pair,
    dec,
    up_stage,
    parts,
    down_stage,
    total_stage,
    total_in,
    next_stage,
    enter_in,
    tot_send,
    tot_recv,
    pair_send,
    pair_recv,
    up_send,
    up_recv,
    down_send,
    down_recv,
    total_send,
    total_recv,
    next_send,
    enter_recv,
    keep_sem,
    load_sem,
    x_sem,
):
    heads = step_ref.shape[1]
    width = x_ref.shape[1]
    own = width // ways
    depth = own // PIECE
    me, seq = lax.axis_index("head"), lax.axis_index("seq")
    core, chip = lax.rem(seq, 2), seq // 2
    chips = seqs // 2
    first = chip == 0

    def peer(q):
        return (seq, q)

    def other(i):
        return lax.rem(me + i, ways)

    def remote(src, dst, send, recv, device):
        return pltpu.make_async_remote_copy(
            src_ref=src,
            dst_ref=dst,
            send_sem=send,
            recv_sem=recv,
            device_id=device,
            device_id_type=MESH,
        )

    def load(i):
        src = (decay_hbm, step_hbm, inject_hbm, readout_hbm)[i]
        dst = (decay_ref, step_ref, inject_ref, readout_ref)[i]
        return pltpu.make_async_copy(src, dst, load_sem.at[i])

    def columns_of(index):
        return pl.ds(pl.multiple_of(index * PIECE, PIECE), PIECE)

    def load_x(index):
        columns = columns_of(index)
        return pltpu.make_async_copy(x_hbm.at[:, columns], x_ref.at[:, columns], x_sem.at[index])

    def place(t):
        return lax.rem(me + 1 + lax.rem(t, ways), ways) * depth + t // ways

    barrier = pltpu.get_barrier_semaphore()

    def greet(device):
        pl.semaphore_signal(barrier, inc=1, device_id=device, device_id_type=MESH)

    for i in range(1, ways):
        greet(peer(other(i)))

    @pl.when(core == 1)
    def _():
        greet((seq - 1, me))

    @pl.when((core == 1) & (chip > 0))
    def _():
        greet((seq - 2, me))

    @pl.when((core == 0) & (chip > 0))
    def _():
        greet((seq - 1, me))

    for i in range(3):
        load(i).start()

    def begin(t, carry):
        load_x(place(t)).start()
        return carry

    lax.fori_loop(0, depth * ways, begin, 0)
    load(3).start()

    load(0).wait()
    load(1).wait()
    (u0, w0, m0, e0), (u1, w1, m1, e1) = factors(step_ref, decay_ref)
    fac[...] = split(
        jnp.concatenate([u0, u1, pad8([jnp.exp(e0 - m0 + e1), jnp.exp(e1 - m1)])], axis=0)
    )
    aux = [jnp.exp(m0), jnp.exp(m1 + e0), jnp.exp(m1 + e0 - m0), skip_ref[...]]
    fac_out[...] = split(jnp.concatenate([w0, w1, pad8(aux)], axis=0))
    tot[me] = jnp.broadcast_to(e0 + e1, (8, heads))

    @pl.when(first)
    def _():
        enter_in[...] = jnp.zeros_like(enter_in)

    ahead = 2 - 2 * (chip // (chips - 1)) if chips > 1 else 0
    pl.semaphore_wait(barrier, ways - core + core * ahead)

    def tot_copy(q):
        return remote(tot.at[me], tot.at[me], tot_send.at[q], tot_recv.at[me], peer(q))

    def tot_from(q):
        return remote(tot.at[q], tot.at[q], tot_send.at[q], tot_recv.at[q], peer(q))

    def up_copy(k, q):
        return remote(
            up_stage.at[k, q], parts.at[k, me], up_send.at[k, q], up_recv.at[k, me], peer(q)
        )

    def up_from(k, q):
        return remote(
            up_stage.at[k, q], parts.at[k, q], up_send.at[k, q], up_recv.at[k, q], peer(q)
        )

    def down_copy(k, q):
        return remote(
            down_stage.at[k, q],
            held_ref.at[me * depth + k],
            down_send.at[k, q],
            down_recv.at[k, me],
            peer(q),
        )

    def down_from(k, q):
        return remote(
            down_stage.at[k, q],
            held_ref.at[q * depth + k],
            down_send.at[k, q],
            down_recv.at[k, q],
            peer(q),
        )

    def keep_copy(k):
        return pltpu.make_async_copy(
            down_stage.at[k, me], held_ref.at[me * depth + k], keep_sem.at[k]
        )

    def pair_copy():
        return remote(pair.at[0], pair.at[1], pair_send, pair_recv, (seq + 1, me))

    def total_copy(k):
        return remote(
            total_stage.at[k], total_in.at[k], total_send.at[k], total_recv.at[k], (seq + 1, me)
        )

    def next_copy(k, ahead):
        return remote(
            next_stage.at[k],
            enter_in.at[k],
            next_send.at[k, ahead - 1],
            enter_recv.at[k],
            (seq + ahead, me),
        )

    for i in range(1, ways):
        tot_copy(other(i)).start()

    def piece(t, carry):
        k, i = t // ways, lax.rem(t, ways)
        q = lax.rem(me + 1 + i, ways)
        index = q * depth + k
        columns = columns_of(index)
        group = index * PIECE // (width // GROUPS)
        shared = pl.ds(pl.multiple_of(group * STATE, STATE), STATE)
        load_x(index).wait()
        wide = dot(fac[...], spread(index, heads, PIECE))
        state = None
        for c in range(2):
            rows = slice(c * CHUNK, (c + 1) * CHUNK)
            drive = (wide[rows] * x_ref[rows, columns].astype(F32)).astype(BF16)
            drive_ref[rows, columns] = drive
            part = dot_rows(inject_ref[rows, shared], drive)
            if c == 0:
                first_state[index] = part
            part = part * wide[2 * CHUNK + c : 2 * CHUNK + c + 1]
            state = part if state is None else state + part

        @pl.when(i == ways - 1)
        def _():
            parts[k, me] = state.astype(BF16)

        @pl.when(i < ways - 1)
        def _():
            up_stage[k, q] = state.astype(BF16)
            up_copy(k, q).start()

        return carry

    load(2).wait()
    lax.fori_loop(0, depth * ways, piece, 0)

    for i in range(1, ways):
        tot_from(other(i)).wait_recv()
    logs = [tot[j][:1] for j in range(ways)]
    whole = sum(logs[1:], logs[0])

    @pl.when(core == 0)
    def _():
        pair[0] = jnp.broadcast_to(whole, (8, heads))
        pair_copy().start()
        pair[1] = jnp.zeros((8, heads), F32)

    @pl.when(core == 1)
    def _():
        pair_copy().wait_recv()

    rows = [jnp.exp(a) for a in logs] + [jnp.exp(pair[1][:1])]
    rows = split(jnp.concatenate(rows + [jnp.zeros_like(rows[0])] * (-len(rows) % 16), axis=0))
    for k in range(depth):
        dec[k] = dot(rows, spread(me * depth + k, heads, PIECE))

    def await_parts(k):
        for i in range(1, ways):
            up_from(k, other(i)).wait_recv()

    def onward(k, running, j):
        return running * dec[k, j : j + 1, :] + parts[k, j].astype(F32)

    def returns(k, running):
        for j in range(ways):
            down_stage[k, j] = running.astype(BF16)
            running = onward(k, running, j)
        return running

    def send_down(k):
        for i in range(1, ways):
            down_copy(k, other(i)).start()
        keep_copy(k).start()

    def await_enter(k):
        @pl.when(chip > 0)
        def _():
            next_copy(k, 1).wait_recv()

    @pl.when(core == 0)
    def _():
        def totals(k):
            await_parts(k)
            running = parts[k, 0].astype(F32)
            for j in range(1, ways):
                running = onward(k, running, j)
            total_stage[k] = running.astype(BF16)
            total_copy(k).start()

        def finish(k):
            await_enter(k)
            returns(k, enter_in[k].astype(F32))
            send_down(k)

        def both(t, carry):
            @pl.when(t < depth)
            def _():
                totals(t)

            @pl.when(t >= BEHIND)
            def _():
                finish(t - BEHIND)

            return carry

        lax.fori_loop(0, depth + BEHIND, both, 0)

    @pl.when(core == 1)
    def _():
        def finish(k, carry):
            await_parts(k)
            total_copy(k).wait_recv()
            await_enter(k)
            start = enter_in[k].astype(F32) * dec[k, ways : ways + 1, :]
            running = returns(k, start + total_in[k].astype(F32))

            @pl.when(chip < chips - 1)
            def _():
                next_stage[k] = running.astype(BF16)
                next_copy(k, 2).start()
                next_copy(k, 1).start()

            send_down(k)
            return carry

        lax.fori_loop(0, depth, finish, 0)

    load(3).wait()
    mask = lower(CHUNK)

    def prepare(index, carry):
        columns = columns_of(index)
        after_ref[:, columns] = dot(fac_out[...], spread(index, heads, PIECE))
        return carry

    def cross(group, carry):
        shared = pl.ds(pl.multiple_of(group * STATE, STATE), STATE)
        for c in range(2):
            rows = slice(c * CHUNK, (c + 1) * CHUNK)
            readout = readout_ref[rows, shared]
            both = dot_last(readout, inject_ref[rows, shared])
            left_ref[group, rows, :CHUNK] = jnp.where(mask, both, 0.0).astype(BF16)
            left_ref[group, rows, CHUNK:] = readout
        return carry

    lax.fori_loop(0, GROUPS, cross, 0)
    lax.fori_loop(0, width // PIECE, prepare, 0)

    def result(k, q):
        index = q * depth + k
        columns = columns_of(index)
        group = index * PIECE // (width // GROUPS)
        held = held_ref[index].astype(F32)
        rest = after_ref[2 * CHUNK : 2 * CHUNK + 8, columns]
        enter = held * rest[0:1]
        for c in range(2):
            rows = slice(c * CHUNK, (c + 1) * CHUNK)
            right = jnp.concatenate([drive_ref[rows, columns], enter.astype(BF16)], axis=0)
            acc = dot(left_ref[group, rows, :], right)
            plain = rest[3:4] * x_ref[rows, columns].astype(F32)
            out_ref[rows, columns] = (after_ref[rows, columns] * acc + plain).astype(BF16)
            if c == 0:
                enter = held * rest[1:2] + first_state[index] * rest[2:3]

    def results(t, carry):
        k, i = t // ways, lax.rem(t, ways)
        q = lax.rem(me + i, ways)

        @pl.when(i == 0)
        def _():
            keep_copy(k).wait()

            @pl.when(k > 0)
            def _():
                for j in range(1, ways):
                    down_copy(k - 1, other(j)).wait_send()

        @pl.when(i > 0)
        def _():
            down_from(k, q).wait_recv()

        result(k, q)
        return carry

    def drain(k, carry):
        for i in range(1, ways):
            up_copy(k, other(i)).wait_send()

        @pl.when(core == 0)
        def _():
            total_copy(k).wait_send()

        @pl.when((core == 1) & (chip < chips - 1))
        def _():
            next_copy(k, 2).wait_send()
            next_copy(k, 1).wait_send()

        return carry

    lax.fori_loop(0, depth, drain, 0)
    for i in range(1, ways):
        tot_copy(other(i)).wait_send()

    @pl.when(core == 0)
    def _():
        pair_copy().wait_send()

    lax.fori_loop(0, depth * ways, results, 0)

    for i in range(1, ways):
        down_copy(depth - 1, other(i)).wait_send()


def store_kernel(mixed_ref, out_hbm, sem):
    rows = mixed_ref.shape[0] // STORES
    copies = []
    for i in range(STORES):
        part = pl.ds(i * rows, rows)
        copies.append(pltpu.make_async_copy(mixed_ref.at[part], out_hbm.at[part], sem.at[i]))
    for copy in copies:
        copy.start()
    for copy in copies:
        copy.wait()


def shards(features, step_size, log_decay, inject, readout, skip_gain):
    ways, seqs = lax.axis_size("head"), lax.axis_size("seq")
    tokens, width = features.shape
    heads = step_size.shape[1]
    depth = width // ways // PIECE
    pieces = width // PIECE
    vmem = pl.BlockSpec(memory_space=pltpu.VMEM)
    dma = pltpu.SemaphoreType.DMA
    mixed = pl.pallas_call(
        functools.partial(mixer_kernel, ways, seqs),
        in_specs=[pl.BlockSpec(memory_space=pltpu.HBM)] * 5 + [vmem],
        out_specs=vmem,
        out_shape=pltpu.VMEM((tokens, width), BF16),
        scratch_shapes=[
            pltpu.VMEM((tokens, width), BF16),
            pltpu.VMEM((tokens, heads), F32),
            pltpu.VMEM((tokens, heads), F32),
            pltpu.VMEM((tokens, GROUPS * STATE), BF16),
            pltpu.VMEM((tokens, GROUPS * STATE), BF16),
            pltpu.VMEM((pieces, STATE, PIECE), BF16),
            pltpu.VMEM((tokens, width), BF16),
            pltpu.VMEM((pieces, STATE, PIECE), F32),
            pltpu.VMEM((tokens + 16, width), F32),
            pltpu.VMEM((GROUPS, tokens, CHUNK + STATE), BF16),
            pltpu.VMEM((2 * CHUNK + 16, 2 * heads), BF16),
            pltpu.VMEM((2 * CHUNK + 16, 2 * heads), BF16),
            pltpu.VMEM((ways, 8, heads), F32),
            pltpu.VMEM((2, 8, heads), F32),
            pltpu.VMEM((depth, (ways + 16) // 16 * 16, PIECE), F32),
            pltpu.VMEM((depth, ways, STATE, PIECE), BF16),
            pltpu.VMEM((depth, ways, STATE, PIECE), BF16),
            pltpu.VMEM((depth, ways, STATE, PIECE), BF16),
            pltpu.VMEM((depth, STATE, PIECE), BF16),
            pltpu.VMEM((depth, STATE, PIECE), BF16),
            pltpu.VMEM((depth, STATE, PIECE), BF16),
            pltpu.VMEM((depth, STATE, PIECE), BF16),
            dma((ways,)),
            dma((ways,)),
            dma,
            dma,
            dma((depth, ways)),
            dma((depth, ways)),
            dma((depth, ways)),
            dma((depth, ways)),
            dma((depth,)),
            dma((depth,)),
            dma((depth, 2)),
            dma((depth,)),
            dma((depth,)),
            dma((4,)),
            dma((pieces,)),
        ],
        compiler_params=pltpu.CompilerParams(
            vmem_limit_bytes=59 * 2**20, collective_id=0, has_side_effects=True
        ),
    )(features, step_size, log_decay, inject, readout, skip_gain[None])
    return pl.pallas_call(
        store_kernel,
        in_specs=[vmem],
        out_specs=pl.BlockSpec(memory_space=pltpu.HBM),
        out_shape=jax.ShapeDtypeStruct((tokens, width), BF16),
        scratch_shapes=[dma((STORES,))],
    )(mixed)


def solution(mesh):
    rows = P(("seq", "head"), None)
    return jax.shard_map(
        shards,
        mesh=mesh,
        in_specs=(rows, rows, rows, rows, rows, P()),
        out_specs=rows,
        check_vma=False,
    )
```

```python
import functools

import jax
import jax.numpy as jnp
from jax import lax
from jax.experimental import pallas as pl
from jax.experimental.pallas import tpu as pltpu
from jax.sharding import PartitionSpec as P

HEAD_DIM = 64
STATE = 128
GROUPS = 8
CHUNK = 128
PIECE = 512
BEHIND = 2
MESH = pl.DeviceIdType.MESH
F32 = jnp.float32
BF16 = jnp.bfloat16


def dot(a, b):
    return jnp.dot(a, b, preferred_element_type=F32)


def dot_rows(a, b):
    return lax.dot_general(a, b, (((0,), (0,)), ((), ())), preferred_element_type=F32)


def dot_last(a, b):
    return lax.dot_general(a, b, (((1,), (1,)), ((), ())), preferred_element_type=F32)


def lower(size):
    return lax.broadcasted_iota(jnp.int32, (size, size), 0) >= lax.broadcasted_iota(
        jnp.int32, (size, size), 1
    )


def cumulative(decay):
    ones = jnp.where(lower(CHUNK), 1.0, 0.0).astype(BF16)
    high = decay.astype(BF16)
    rest = decay - high.astype(F32)
    mid = rest.astype(BF16)
    low = (rest - mid.astype(F32)).astype(BF16)
    return dot(ones, high) + dot(ones, mid) + dot(ones, low)


def split(x):
    high = x.astype(BF16)
    return jnp.concatenate([high, (x - high.astype(F32)).astype(BF16)], axis=1)


def spread(group, heads, columns):
    head = lax.broadcasted_iota(jnp.int32, (2 * heads, columns), 0)
    head = jnp.where(head >= heads, head - heads, head)
    column = lax.broadcasted_iota(jnp.int32, (2 * heads, columns), 1)
    first = (head - group * (columns // HEAD_DIM)) * HEAD_DIM
    return jnp.where((column >= first) & (column < first + HEAD_DIM), 1.0, 0.0).astype(BF16)


def factors(step_ref, decay_ref):
    half = CHUNK // 2 - 1
    out = []
    for c in range(2):
        rows = pl.ds(c * CHUNK, CHUNK)
        cum = cumulative(decay_ref[rows, :])
        mid, end = cum[half : half + 1], cum[CHUNK - 1 : CHUNK]
        out.append((step_ref[rows, :] * jnp.exp(mid - cum), jnp.exp(cum - mid), mid, end))
    return out


def pad8(rows):
    rows = list(rows)
    return jnp.concatenate(rows + [jnp.zeros_like(rows[0])] * (16 - len(rows)), axis=0)


def mixer_kernel(
    ways,
    seqs,
    x_hbm,
    step_hbm,
    decay_hbm,
    inject_hbm,
    readout_hbm,
    skip_ref,
    out_ref,
    x_ref,
    step_ref,
    decay_ref,
    inject_ref,
    readout_ref,
    held_ref,
    drive_ref,
    first_state,
    after_ref,
    left_ref,
    fac,
    fac_out,
    tot,
    pair,
    dec,
    up_stage,
    parts,
    down_stage,
    total_stage,
    total_in,
    next_stage,
    enter_in,
    tot_send,
    tot_recv,
    pair_send,
    pair_recv,
    up_send,
    up_recv,
    down_send,
    down_recv,
    total_send,
    total_recv,
    next_send,
    enter_recv,
    keep_sem,
    load_sem,
    x_sem,
):
    heads = step_ref.shape[1]
    width = x_ref.shape[1]
    own = width // ways
    depth = own // PIECE
    me, seq = lax.axis_index("head"), lax.axis_index("seq")
    core, chip = lax.rem(seq, 2), seq // 2
    chips = seqs // 2
    first = chip == 0

    def peer(q):
        return (seq, q)

    def other(i):
        return lax.rem(me + i, ways)

    def remote(src, dst, send, recv, device):
        return pltpu.make_async_remote_copy(
            src_ref=src,
            dst_ref=dst,
            send_sem=send,
            recv_sem=recv,
            device_id=device,
            device_id_type=MESH,
        )

    def load(i):
        src = (decay_hbm, step_hbm, inject_hbm, readout_hbm)[i]
        dst = (decay_ref, step_ref, inject_ref, readout_ref)[i]
        return pltpu.make_async_copy(src, dst, load_sem.at[i])

    def columns_of(index):
        return pl.ds(pl.multiple_of(index * PIECE, PIECE), PIECE)

    def load_x(index):
        columns = columns_of(index)
        return pltpu.make_async_copy(x_hbm.at[:, columns], x_ref.at[:, columns], x_sem.at[index])

    def place(t):
        return lax.rem(me + 1 + lax.rem(t, ways), ways) * depth + t // ways

    barrier = pltpu.get_barrier_semaphore()

    def greet(device):
        pl.semaphore_signal(barrier, inc=1, device_id=device, device_id_type=MESH)

    for i in range(1, ways):
        greet(peer(other(i)))

    @pl.when(core == 1)
    def _():
        greet((seq - 1, me))

    @pl.when((core == 1) & (chip > 0))
    def _():
        greet((seq - 2, me))

    @pl.when((core == 0) & (chip > 0))
    def _():
        greet((seq - 1, me))

    for i in range(3):
        load(i).start()

    def begin(t, carry):
        load_x(place(t)).start()
        return carry

    lax.fori_loop(0, depth * ways, begin, 0)
    load(3).start()

    load(0).wait()
    load(1).wait()
    (u0, w0, m0, e0), (u1, w1, m1, e1) = factors(step_ref, decay_ref)
    fac[...] = split(
        jnp.concatenate([u0, u1, pad8([jnp.exp(e0 - m0 + e1), jnp.exp(e1 - m1)])], axis=0)
    )
    aux = [jnp.exp(m0), jnp.exp(m1 + e0), jnp.exp(m1 + e0 - m0), skip_ref[...]]
    fac_out[...] = split(jnp.concatenate([w0, w1, pad8(aux)], axis=0))
    tot[me] = jnp.broadcast_to(e0 + e1, (8, heads))

    @pl.when(first)
    def _():
        enter_in[...] = jnp.zeros_like(enter_in)

    def tot_copy(q):
        return remote(tot.at[me], tot.at[me], tot_send.at[q], tot_recv.at[me], peer(q))

    def tot_from(q):
        return remote(tot.at[q], tot.at[q], tot_send.at[q], tot_recv.at[q], peer(q))

    def up_copy(k, q):
        return remote(
            up_stage.at[k, q], parts.at[k, me], up_send.at[k, q], up_recv.at[k, me], peer(q)
        )

    def up_from(k, q):
        return remote(
            up_stage.at[k, q], parts.at[k, q], up_send.at[k, q], up_recv.at[k, q], peer(q)
        )

    def down_copy(k, q):
        return remote(
            down_stage.at[k, q],
            held_ref.at[me * depth + k],
            down_send.at[k, q],
            down_recv.at[k, me],
            peer(q),
        )

    def down_from(k, q):
        return remote(
            down_stage.at[k, q],
            held_ref.at[q * depth + k],
            down_send.at[k, q],
            down_recv.at[k, q],
            peer(q),
        )

    def keep_copy(k):
        return pltpu.make_async_copy(
            down_stage.at[k, me], held_ref.at[me * depth + k], keep_sem.at[k]
        )

    def pair_copy():
        return remote(pair.at[0], pair.at[1], pair_send, pair_recv, (seq + 1, me))

    def total_copy(k):
        return remote(
            total_stage.at[k], total_in.at[k], total_send.at[k], total_recv.at[k], (seq + 1, me)
        )

    def next_copy(k, ahead):
        return remote(
            next_stage.at[k],
            enter_in.at[k],
            next_send.at[k, ahead - 1],
            enter_recv.at[k],
            (seq + ahead, me),
        )

    def piece(t):
        k, i = t // ways, lax.rem(t, ways)
        q = lax.rem(me + 1 + i, ways)
        index = q * depth + k
        columns = columns_of(index)
        group = index * PIECE // (width // GROUPS)
        shared = pl.ds(pl.multiple_of(group * STATE, STATE), STATE)
        load_x(index).wait()
        wide = dot(fac[...], spread(index, heads, PIECE))
        state = None
        for c in range(2):
            rows = slice(c * CHUNK, (c + 1) * CHUNK)
            drive = (wide[rows] * x_ref[rows, columns].astype(F32)).astype(BF16)
            drive_ref[rows, columns] = drive
            part = dot_rows(inject_ref[rows, shared], drive)
            if c == 0:
                first_state[index] = part
            part = part * wide[2 * CHUNK + c : 2 * CHUNK + c + 1]
            state = part if state is None else state + part

        @pl.when(i == ways - 1)
        def _():
            parts[k, me] = state.astype(BF16)

        @pl.when(i < ways - 1)
        def _():
            up_stage[k, q] = state.astype(BF16)

    def pass_on(t):
        k, i = t // ways, lax.rem(t, ways)

        @pl.when(i < ways - 1)
        def _():
            up_copy(k, lax.rem(me + 1 + i, ways)).start()

    def step(t, carry):
        piece(t)
        pass_on(t)
        return carry

    load(2).wait()
    piece(0)
    ahead = 2 - 2 * (chip // (chips - 1)) if chips > 1 else 0
    pl.semaphore_wait(barrier, ways - core + core * ahead)

    pass_on(0)
    for i in range(1, ways):
        tot_copy(other(i)).start()

    lax.fori_loop(1, depth * ways, step, 0)

    for i in range(1, ways):
        tot_from(other(i)).wait_recv()
    logs = [tot[j][:1] for j in range(ways)]
    whole = sum(logs[1:], logs[0])

    @pl.when(core == 0)
    def _():
        pair[0] = jnp.broadcast_to(whole, (8, heads))
        pair_copy().start()
        pair[1] = jnp.zeros((8, heads), F32)

    @pl.when(core == 1)
    def _():
        pair_copy().wait_recv()

    rows = [jnp.exp(a) for a in logs] + [jnp.exp(pair[1][:1])]
    rows = split(jnp.concatenate(rows + [jnp.zeros_like(rows[0])] * (-len(rows) % 16), axis=0))
    for k in range(depth):
        dec[k] = dot(rows, spread(me * depth + k, heads, PIECE))

    def await_parts(k):
        for i in range(1, ways):
            up_from(k, other(i)).wait_recv()

    def onward(k, running, j):
        return running * dec[k, j : j + 1, :] + parts[k, j].astype(F32)

    def returns(k, running):
        for j in range(ways):
            down_stage[k, j] = running.astype(BF16)
            running = onward(k, running, j)
        return running

    def send_down(k):
        for i in range(1, ways):
            down_copy(k, other(i)).start()
        keep_copy(k).start()

    def await_enter(k):
        @pl.when(chip > 0)
        def _():
            next_copy(k, 1).wait_recv()

    @pl.when(core == 0)
    def _():
        def totals(k):
            await_parts(k)
            running = parts[k, 0].astype(F32)
            for j in range(1, ways):
                running = onward(k, running, j)
            total_stage[k] = running.astype(BF16)
            total_copy(k).start()

        def finish(k):
            await_enter(k)
            returns(k, enter_in[k].astype(F32))
            send_down(k)

        def both(t, carry):
            @pl.when(t < depth)
            def _():
                totals(t)

            @pl.when(t >= BEHIND)
            def _():
                finish(t - BEHIND)

            return carry

        lax.fori_loop(0, depth + BEHIND, both, 0)

    @pl.when(core == 1)
    def _():
        def finish(k, carry):
            await_parts(k)
            total_copy(k).wait_recv()
            await_enter(k)
            start = enter_in[k].astype(F32) * dec[k, ways : ways + 1, :]
            running = returns(k, start + total_in[k].astype(F32))

            @pl.when(chip < chips - 1)
            def _():
                next_stage[k] = running.astype(BF16)
                next_copy(k, 2).start()
                next_copy(k, 1).start()

            send_down(k)
            return carry

        lax.fori_loop(0, depth, finish, 0)

    load(3).wait()
    mask = lower(CHUNK)

    def prepare(index, carry):
        columns = columns_of(index)
        after_ref[:, columns] = dot(fac_out[...], spread(index, heads, PIECE))
        return carry

    def cross(group, carry):
        shared = pl.ds(pl.multiple_of(group * STATE, STATE), STATE)
        for c in range(2):
            rows = slice(c * CHUNK, (c + 1) * CHUNK)
            readout = readout_ref[rows, shared]
            both = dot_last(readout, inject_ref[rows, shared])
            left_ref[group, rows, :CHUNK] = jnp.where(mask, both, 0.0).astype(BF16)
            left_ref[group, rows, CHUNK:] = readout
        return carry

    lax.fori_loop(0, GROUPS, cross, 0)
    lax.fori_loop(0, width // PIECE, prepare, 0)

    def result(k, q):
        index = q * depth + k
        columns = columns_of(index)
        group = index * PIECE // (width // GROUPS)
        held = held_ref[index].astype(F32)
        rest = after_ref[2 * CHUNK : 2 * CHUNK + 8, columns]
        enter = held * rest[0:1]
        for c in range(2):
            rows = slice(c * CHUNK, (c + 1) * CHUNK)
            right = jnp.concatenate([drive_ref[rows, columns], enter.astype(BF16)], axis=0)
            acc = dot(left_ref[group, rows, :], right)
            plain = rest[3:4] * x_ref[rows, columns].astype(F32)
            out_ref[rows, columns] = (after_ref[rows, columns] * acc + plain).astype(BF16)
            if c == 0:
                enter = held * rest[1:2] + first_state[index] * rest[2:3]

    def results(t, carry):
        k, i = t // ways, lax.rem(t, ways)
        q = lax.rem(me + i, ways)

        @pl.when(i == 0)
        def _():
            keep_copy(k).wait()

            @pl.when(k > 0)
            def _():
                for j in range(1, ways):
                    down_copy(k - 1, other(j)).wait_send()

        @pl.when(i > 0)
        def _():
            down_from(k, q).wait_recv()

        result(k, q)
        return carry

    def drain(k, carry):
        for i in range(1, ways):
            up_copy(k, other(i)).wait_send()

        @pl.when(core == 0)
        def _():
            total_copy(k).wait_send()

        @pl.when((core == 1) & (chip < chips - 1))
        def _():
            next_copy(k, 2).wait_send()
            next_copy(k, 1).wait_send()

        return carry

    lax.fori_loop(0, depth, drain, 0)
    for i in range(1, ways):
        tot_copy(other(i)).wait_send()

    @pl.when(core == 0)
    def _():
        pair_copy().wait_send()

    lax.fori_loop(0, depth * ways, results, 0)

    for i in range(1, ways):
        down_copy(depth - 1, other(i)).wait_send()


def shards(features, step_size, log_decay, inject, readout, skip_gain):
    ways, seqs = lax.axis_size("head"), lax.axis_size("seq")
    tokens, width = features.shape
    heads = step_size.shape[1]
    depth = width // ways // PIECE
    pieces = width // PIECE
    vmem = pl.BlockSpec(memory_space=pltpu.VMEM)
    dma = pltpu.SemaphoreType.DMA
    return pl.pallas_call(
        functools.partial(mixer_kernel, ways, seqs),
        in_specs=[pl.BlockSpec(memory_space=pltpu.HBM)] * 5 + [vmem],
        out_specs=vmem,
        out_shape=pltpu.VMEM((tokens, width), BF16),
        scratch_shapes=[
            pltpu.VMEM((tokens, width), BF16),
            pltpu.VMEM((tokens, heads), F32),
            pltpu.VMEM((tokens, heads), F32),
            pltpu.VMEM((tokens, GROUPS * STATE), BF16),
            pltpu.VMEM((tokens, GROUPS * STATE), BF16),
            pltpu.VMEM((pieces, STATE, PIECE), BF16),
            pltpu.VMEM((tokens, width), BF16),
            pltpu.VMEM((pieces, STATE, PIECE), F32),
            pltpu.VMEM((tokens + 16, width), F32),
            pltpu.VMEM((GROUPS, tokens, CHUNK + STATE), BF16),
            pltpu.VMEM((2 * CHUNK + 16, 2 * heads), BF16),
            pltpu.VMEM((2 * CHUNK + 16, 2 * heads), BF16),
            pltpu.VMEM((ways, 8, heads), F32),
            pltpu.VMEM((2, 8, heads), F32),
            pltpu.VMEM((depth, (ways + 16) // 16 * 16, PIECE), F32),
            pltpu.VMEM((depth, ways, STATE, PIECE), BF16),
            pltpu.VMEM((depth, ways, STATE, PIECE), BF16),
            pltpu.VMEM((depth, ways, STATE, PIECE), BF16),
            pltpu.VMEM((depth, STATE, PIECE), BF16),
            pltpu.VMEM((depth, STATE, PIECE), BF16),
            pltpu.VMEM((depth, STATE, PIECE), BF16),
            pltpu.VMEM((depth, STATE, PIECE), BF16),
            dma((ways,)),
            dma((ways,)),
            dma,
            dma,
            dma((depth, ways)),
            dma((depth, ways)),
            dma((depth, ways)),
            dma((depth, ways)),
            dma((depth,)),
            dma((depth,)),
            dma((depth, 2)),
            dma((depth,)),
            dma((depth,)),
            dma((4,)),
            dma((pieces,)),
        ],
        compiler_params=pltpu.CompilerParams(
            vmem_limit_bytes=59 * 2**20, collective_id=0, has_side_effects=True
        ),
    )(features, step_size, log_decay, inject, readout, skip_gain[None])


def solution(mesh):
    rows = P(("seq", "head"), None)
    return jax.shard_map(
        shards,
        mesh=mesh,
        in_specs=(rows, rows, rows, rows, rows, P()),
        out_specs=rows,
        check_vma=False,
    )
```

```python
import functools

import jax
import jax.numpy as jnp
from jax import lax
from jax.experimental import pallas as pl
from jax.experimental.pallas import tpu as pltpu
from jax.sharding import PartitionSpec as P

HEAD_DIM = 64
STATE = 128
GROUPS = 8
CHUNK = 128
PIECE = 512
BEHIND = 1
MESH = pl.DeviceIdType.MESH
F32 = jnp.float32
BF16 = jnp.bfloat16


def dot(a, b):
    return jnp.dot(a, b, preferred_element_type=F32)


def dot_rows(a, b):
    return lax.dot_general(a, b, (((0,), (0,)), ((), ())), preferred_element_type=F32)


def dot_last(a, b):
    return lax.dot_general(a, b, (((1,), (1,)), ((), ())), preferred_element_type=F32)


def lower(size):
    return lax.broadcasted_iota(jnp.int32, (size, size), 0) >= lax.broadcasted_iota(
        jnp.int32, (size, size), 1
    )


def cumulative(decay):
    ones = jnp.where(lower(CHUNK), 1.0, 0.0).astype(BF16)
    high = decay.astype(BF16)
    rest = decay - high.astype(F32)
    mid = rest.astype(BF16)
    low = (rest - mid.astype(F32)).astype(BF16)
    return dot(ones, high) + dot(ones, mid) + dot(ones, low)


def split(x):
    high = x.astype(BF16)
    return jnp.concatenate([high, (x - high.astype(F32)).astype(BF16)], axis=1)


def spread(group, heads, columns):
    head = lax.broadcasted_iota(jnp.int32, (2 * heads, columns), 0)
    head = jnp.where(head >= heads, head - heads, head)
    column = lax.broadcasted_iota(jnp.int32, (2 * heads, columns), 1)
    first = (head - group * (columns // HEAD_DIM)) * HEAD_DIM
    return jnp.where((column >= first) & (column < first + HEAD_DIM), 1.0, 0.0).astype(BF16)


def factors(step_ref, decay_ref):
    half = CHUNK // 2 - 1
    out = []
    for c in range(2):
        rows = pl.ds(c * CHUNK, CHUNK)
        cum = cumulative(decay_ref[rows, :])
        mid, end = cum[half : half + 1], cum[CHUNK - 1 : CHUNK]
        out.append((step_ref[rows, :] * jnp.exp(mid - cum), jnp.exp(cum - mid), mid, end))
    return out


def pad8(rows):
    rows = list(rows)
    return jnp.concatenate(rows + [jnp.zeros_like(rows[0])] * (16 - len(rows)), axis=0)


def mixer_kernel(
    ways,
    seqs,
    x_hbm,
    step_hbm,
    decay_hbm,
    inject_hbm,
    readout_hbm,
    skip_ref,
    out_ref,
    x_ref,
    step_ref,
    decay_ref,
    inject_ref,
    readout_ref,
    held_ref,
    drive_ref,
    first_state,
    after_ref,
    left_ref,
    fac,
    fac_out,
    tot,
    pair,
    dec,
    up_stage,
    parts,
    down_stage,
    total_stage,
    total_in,
    next_stage,
    enter_in,
    tot_send,
    tot_recv,
    pair_send,
    pair_recv,
    up_send,
    up_recv,
    down_send,
    down_recv,
    total_send,
    total_recv,
    next_send,
    enter_recv,
    keep_sem,
    load_sem,
    x_sem,
):
    heads = step_ref.shape[1]
    width = x_ref.shape[1]
    own = width // ways
    depth = own // PIECE
    me, seq = lax.axis_index("head"), lax.axis_index("seq")
    core, chip = lax.rem(seq, 2), seq // 2
    chips = seqs // 2
    first = chip == 0

    def peer(q):
        return (seq, q)

    def other(i):
        return lax.rem(me + i, ways)

    def remote(src, dst, send, recv, device):
        return pltpu.make_async_remote_copy(
            src_ref=src,
            dst_ref=dst,
            send_sem=send,
            recv_sem=recv,
            device_id=device,
            device_id_type=MESH,
        )

    def load(i):
        src = (decay_hbm, step_hbm, inject_hbm, readout_hbm)[i]
        dst = (decay_ref, step_ref, inject_ref, readout_ref)[i]
        return pltpu.make_async_copy(src, dst, load_sem.at[i])

    def columns_of(index):
        return pl.ds(pl.multiple_of(index * PIECE, PIECE), PIECE)

    def load_x(index):
        columns = columns_of(index)
        return pltpu.make_async_copy(x_hbm.at[:, columns], x_ref.at[:, columns], x_sem.at[index])

    def place(t):
        return lax.rem(me + 1 + lax.rem(t, ways), ways) * depth + t // ways

    barrier = pltpu.get_barrier_semaphore()

    def greet(device):
        pl.semaphore_signal(barrier, inc=1, device_id=device, device_id_type=MESH)

    for i in range(1, ways):
        greet(peer(other(i)))

    @pl.when(core == 1)
    def _():
        greet((seq - 1, me))

    @pl.when((core == 1) & (chip > 0))
    def _():
        greet((seq - 2, me))

    @pl.when((core == 0) & (chip > 0))
    def _():
        greet((seq - 1, me))

    for i in range(3):
        load(i).start()

    def begin(t, carry):
        load_x(place(t)).start()
        return carry

    lax.fori_loop(0, depth * ways, begin, 0)
    load(3).start()

    load(0).wait()
    load(1).wait()
    (u0, w0, m0, e0), (u1, w1, m1, e1) = factors(step_ref, decay_ref)
    fac[...] = split(
        jnp.concatenate([u0, u1, pad8([jnp.exp(e0 - m0 + e1), jnp.exp(e1 - m1)])], axis=0)
    )
    aux = [jnp.exp(m0), jnp.exp(m1 + e0), jnp.exp(m1 + e0 - m0), skip_ref[...]]
    fac_out[...] = split(jnp.concatenate([w0, w1, pad8(aux)], axis=0))
    tot[me] = jnp.broadcast_to(e0 + e1, (8, heads))

    @pl.when(first)
    def _():
        enter_in[...] = jnp.zeros_like(enter_in)

    def tot_copy(q):
        return remote(tot.at[me], tot.at[me], tot_send.at[q], tot_recv.at[me], peer(q))

    def tot_from(q):
        return remote(tot.at[q], tot.at[q], tot_send.at[q], tot_recv.at[q], peer(q))

    def up_copy(k, q):
        return remote(
            up_stage.at[k, q], parts.at[k, me], up_send.at[k, q], up_recv.at[k, me], peer(q)
        )

    def up_from(k, q):
        return remote(
            up_stage.at[k, q], parts.at[k, q], up_send.at[k, q], up_recv.at[k, q], peer(q)
        )

    def down_copy(k, q):
        return remote(
            down_stage.at[k, q],
            held_ref.at[me * depth + k],
            down_send.at[k, q],
            down_recv.at[k, me],
            peer(q),
        )

    def down_from(k, q):
        return remote(
            down_stage.at[k, q],
            held_ref.at[q * depth + k],
            down_send.at[k, q],
            down_recv.at[k, q],
            peer(q),
        )

    def keep_copy(k):
        return pltpu.make_async_copy(
            down_stage.at[k, me], held_ref.at[me * depth + k], keep_sem.at[k]
        )

    def pair_copy():
        return remote(pair.at[0], pair.at[1], pair_send, pair_recv, (seq + 1, me))

    def total_copy(k):
        return remote(
            total_stage.at[k], total_in.at[k], total_send.at[k], total_recv.at[k], (seq + 1, me)
        )

    def next_copy(k, ahead):
        return remote(
            next_stage.at[k],
            enter_in.at[k],
            next_send.at[k, ahead - 1],
            enter_recv.at[k],
            (seq + ahead, me),
        )

    def piece(t):
        k, i = t // ways, lax.rem(t, ways)
        q = lax.rem(me + 1 + i, ways)
        index = q * depth + k
        columns = columns_of(index)
        group = index * PIECE // (width // GROUPS)
        shared = pl.ds(pl.multiple_of(group * STATE, STATE), STATE)
        load_x(index).wait()
        wide = dot(fac[...], spread(index, heads, PIECE))
        state = None
        for c in range(2):
            rows = slice(c * CHUNK, (c + 1) * CHUNK)
            drive = (wide[rows] * x_ref[rows, columns].astype(F32)).astype(BF16)
            drive_ref[rows, columns] = drive
            part = dot_rows(inject_ref[rows, shared], drive)
            if c == 0:
                first_state[index] = part
            part = part * wide[2 * CHUNK + c : 2 * CHUNK + c + 1]
            state = part if state is None else state + part

        @pl.when(i == ways - 1)
        def _():
            parts[k, me] = state.astype(BF16)

        @pl.when(i < ways - 1)
        def _():
            up_stage[k, q] = state.astype(BF16)

    def pass_on(t):
        k, i = t // ways, lax.rem(t, ways)

        @pl.when(i < ways - 1)
        def _():
            up_copy(k, lax.rem(me + 1 + i, ways)).start()

    def step(t, carry):
        piece(t)
        pass_on(t)
        return carry

    load(2).wait()
    piece(0)
    ahead = 2 - 2 * (chip // (chips - 1)) if chips > 1 else 0
    pl.semaphore_wait(barrier, ways - core + core * ahead)

    pass_on(0)
    for i in range(1, ways):
        tot_copy(other(i)).start()

    lax.fori_loop(1, depth * ways, step, 0)

    for i in range(1, ways):
        tot_from(other(i)).wait_recv()
    logs = [tot[j][:1] for j in range(ways)]
    whole = sum(logs[1:], logs[0])

    @pl.when(core == 0)
    def _():
        pair[0] = jnp.broadcast_to(whole, (8, heads))
        pair_copy().start()
        pair[1] = jnp.zeros((8, heads), F32)

    @pl.when(core == 1)
    def _():
        pair_copy().wait_recv()

    rows = [jnp.exp(a) for a in logs] + [jnp.exp(pair[1][:1])]
    rows = split(jnp.concatenate(rows + [jnp.zeros_like(rows[0])] * (-len(rows) % 16), axis=0))
    for k in range(depth):
        dec[k] = dot(rows, spread(me * depth + k, heads, PIECE))

    def await_parts(k):
        for i in range(1, ways):
            up_from(k, other(i)).wait_recv()

    def onward(k, running, j):
        return running * dec[k, j : j + 1, :] + parts[k, j].astype(F32)

    def returns(k, running):
        for j in range(ways):
            down_stage[k, j] = running.astype(BF16)
            running = onward(k, running, j)
        return running

    def send_down(k):
        for i in range(1, ways):
            down_copy(k, other(i)).start()
        keep_copy(k).start()

    def await_enter(k):
        @pl.when(chip > 0)
        def _():
            next_copy(k, 1).wait_recv()

    @pl.when(core == 0)
    def _():
        def totals(k):
            await_parts(k)
            running = parts[k, 0].astype(F32)
            for j in range(1, ways):
                running = onward(k, running, j)
            total_stage[k] = running.astype(BF16)
            total_copy(k).start()

        def finish(k):
            await_enter(k)
            returns(k, enter_in[k].astype(F32))
            send_down(k)

        def both(t, carry):
            @pl.when(t < depth)
            def _():
                totals(t)

            @pl.when(t >= BEHIND)
            def _():
                finish(t - BEHIND)

            return carry

        lax.fori_loop(0, depth + BEHIND, both, 0)

    @pl.when(core == 1)
    def _():
        def finish(k, carry):
            await_parts(k)
            total_copy(k).wait_recv()
            await_enter(k)
            start = enter_in[k].astype(F32) * dec[k, ways : ways + 1, :]
            running = returns(k, start + total_in[k].astype(F32))

            @pl.when(chip < chips - 1)
            def _():
                next_stage[k] = running.astype(BF16)
                next_copy(k, 2).start()
                next_copy(k, 1).start()

            send_down(k)
            return carry

        lax.fori_loop(0, depth, finish, 0)

    load(3).wait()
    mask = lower(CHUNK)

    def prepare(index, carry):
        columns = columns_of(index)
        after_ref[:, columns] = dot(fac_out[...], spread(index, heads, PIECE))
        return carry

    def cross(group, carry):
        shared = pl.ds(pl.multiple_of(group * STATE, STATE), STATE)
        for c in range(2):
            rows = slice(c * CHUNK, (c + 1) * CHUNK)
            readout = readout_ref[rows, shared]
            both = dot_last(readout, inject_ref[rows, shared])
            left_ref[group, rows, :CHUNK] = jnp.where(mask, both, 0.0).astype(BF16)
            left_ref[group, rows, CHUNK:] = readout
        return carry

    lax.fori_loop(0, GROUPS, cross, 0)
    lax.fori_loop(0, width // PIECE, prepare, 0)

    def result(k, q):
        index = q * depth + k
        columns = columns_of(index)
        group = index * PIECE // (width // GROUPS)
        held = held_ref[index].astype(F32)
        rest = after_ref[2 * CHUNK : 2 * CHUNK + 8, columns]
        enter = held * rest[0:1]
        for c in range(2):
            rows = slice(c * CHUNK, (c + 1) * CHUNK)
            right = jnp.concatenate([drive_ref[rows, columns], enter.astype(BF16)], axis=0)
            acc = dot(left_ref[group, rows, :], right)
            plain = rest[3:4] * x_ref[rows, columns].astype(F32)
            out_ref[rows, columns] = (after_ref[rows, columns] * acc + plain).astype(BF16)
            if c == 0:
                enter = held * rest[1:2] + first_state[index] * rest[2:3]

    def results(t, carry):
        k, i = t // ways, lax.rem(t, ways)
        q = lax.rem(me + i, ways)

        @pl.when(i == 0)
        def _():
            keep_copy(k).wait()

            @pl.when(k > 0)
            def _():
                for j in range(1, ways):
                    down_copy(k - 1, other(j)).wait_send()

        @pl.when(i > 0)
        def _():
            down_from(k, q).wait_recv()

        result(k, q)
        return carry

    def drain(k, carry):
        for i in range(1, ways):
            up_copy(k, other(i)).wait_send()

        @pl.when(core == 0)
        def _():
            total_copy(k).wait_send()

        @pl.when((core == 1) & (chip < chips - 1))
        def _():
            next_copy(k, 2).wait_send()
            next_copy(k, 1).wait_send()

        return carry

    lax.fori_loop(0, depth, drain, 0)
    for i in range(1, ways):
        tot_copy(other(i)).wait_send()

    @pl.when(core == 0)
    def _():
        pair_copy().wait_send()

    lax.fori_loop(0, depth * ways, results, 0)

    for i in range(1, ways):
        down_copy(depth - 1, other(i)).wait_send()


def shards(features, step_size, log_decay, inject, readout, skip_gain):
    ways, seqs = lax.axis_size("head"), lax.axis_size("seq")
    tokens, width = features.shape
    heads = step_size.shape[1]
    depth = width // ways // PIECE
    pieces = width // PIECE
    vmem = pl.BlockSpec(memory_space=pltpu.VMEM)
    dma = pltpu.SemaphoreType.DMA
    return pl.pallas_call(
        functools.partial(mixer_kernel, ways, seqs),
        in_specs=[pl.BlockSpec(memory_space=pltpu.HBM)] * 5 + [vmem],
        out_specs=vmem,
        out_shape=pltpu.VMEM((tokens, width), BF16),
        scratch_shapes=[
            pltpu.VMEM((tokens, width), BF16),
            pltpu.VMEM((tokens, heads), F32),
            pltpu.VMEM((tokens, heads), F32),
            pltpu.VMEM((tokens, GROUPS * STATE), BF16),
            pltpu.VMEM((tokens, GROUPS * STATE), BF16),
            pltpu.VMEM((pieces, STATE, PIECE), BF16),
            pltpu.VMEM((tokens, width), BF16),
            pltpu.VMEM((pieces, STATE, PIECE), F32),
            pltpu.VMEM((tokens + 16, width), F32),
            pltpu.VMEM((GROUPS, tokens, CHUNK + STATE), BF16),
            pltpu.VMEM((2 * CHUNK + 16, 2 * heads), BF16),
            pltpu.VMEM((2 * CHUNK + 16, 2 * heads), BF16),
            pltpu.VMEM((ways, 8, heads), F32),
            pltpu.VMEM((2, 8, heads), F32),
            pltpu.VMEM((depth, (ways + 16) // 16 * 16, PIECE), F32),
            pltpu.VMEM((depth, ways, STATE, PIECE), BF16),
            pltpu.VMEM((depth, ways, STATE, PIECE), BF16),
            pltpu.VMEM((depth, ways, STATE, PIECE), BF16),
            pltpu.VMEM((depth, STATE, PIECE), BF16),
            pltpu.VMEM((depth, STATE, PIECE), BF16),
            pltpu.VMEM((depth, STATE, PIECE), BF16),
            pltpu.VMEM((depth, STATE, PIECE), BF16),
            dma((ways,)),
            dma((ways,)),
            dma,
            dma,
            dma((depth, ways)),
            dma((depth, ways)),
            dma((depth, ways)),
            dma((depth, ways)),
            dma((depth,)),
            dma((depth,)),
            dma((depth, 2)),
            dma((depth,)),
            dma((depth,)),
            dma((4,)),
            dma((pieces,)),
        ],
        compiler_params=pltpu.CompilerParams(
            vmem_limit_bytes=59 * 2**20, collective_id=0, has_side_effects=True
        ),
    )(features, step_size, log_decay, inject, readout, skip_gain[None])


def solution(mesh):
    rows = P(("seq", "head"), None)
    return jax.shard_map(
        shards,
        mesh=mesh,
        in_specs=(rows, rows, rows, rows, rows, P()),
        out_specs=rows,
        check_vma=False,
    )
```
